256 devices in a mesh: row: 16 (over x, z_lo), col: 4 (over y), depth: 4 (over z_hi, core).
Axes of the slice: x: 4, y: 4, z: 8 (z_hi: 2, z_lo: 4; z = z_hi * 4 + z_lo), core: 2. Of those that a mesh axis runs over, the one named last changes fastest.
Arguments:
- features: bfloat16 [65536, 512], P(('row', 'col'), 'depth'), may hold values from -6 to 6
- weight: bfloat16 [512, 512], replicated, may hold values from -0.25 to 0.25
- cotangent: bfloat16 [65536, 512], P(('row', 'col'), 'depth'), may hold values from -6 to 6
- adjacency_blocks: bfloat16 [16, 4, 80, 256, 256], P('row', 'col'), may hold values from -0.078125 to 0.078125
- block_rows: int32 [16, 4, 80], P('row', 'col'), may hold values from 0 to 15, as said below
- block_cols: int32 [16, 4, 80], P('row', 'col'), may hold values from 0 to 63
- tile_counts: int32 [16, 4], P('row', 'col'), may hold values from 20 to 80, as said below
Outputs:
- activated: bfloat16 [65536, 512], P(('row', 'col'), 'depth')
- grad_features: bfloat16 [65536, 512], P(('row', 'col'), 'depth')
- grad_weight: float32 [512, 512], P('depth')
The draws below stay inside these ranges and needn't reach their ends.
Inputs may be any that keep to these rules, and one draw needn't show every extreme that they name: Within one tile the pairs (block_rows, block_cols) of its 80 slots are all different. `tile_counts`: some tile uses all 80 slots.
All inputs are finite; a program needn't handle non-finite values.
Results may differ from the reference program's by a relative error of at most 0.029.
Values may be sent and summed in bfloat16 or wider, within the bound.
A program may use at most 64 MiB of HBM per device.

```python
import jax
import jax.numpy as jnp
from jax import lax

F = 512
BLOCK = 256
NB = 80
BP = 4
RBT = 16
CBT = 64
NV = 65536
N_ROW = 16
N_COL = 4


def picked_slots(key):
    tile_keys = jax.random.split(key, N_ROW * N_COL)

    def one_tile(tile_key):
        return jax.random.permutation(tile_key, RBT * CBT)[:NB]
    return jax.vmap(one_tile)(tile_keys).reshape(N_ROW, N_COL, NB).astype(jnp.int32)


def draw_block_rows(key, part):
    slots = picked_slots(key)
    return (slots // CBT).astype(jnp.int32)


def draw_block_cols(key, part):
    slots = picked_slots(key)
    return (slots % CBT).astype(jnp.int32)


def draw_tile_counts(key, part):
    key = jax.random.fold_in(key, 3)
    first_key, second_key = jax.random.split(key)
    counts = jax.random.randint(first_key, (N_ROW * N_COL,), max(NB // 4, 1), NB + 1).astype(jnp.int32)
    fullest = jax.random.randint(second_key, (), 0, N_ROW * N_COL)
    counts = counts.at[fullest].set(NB)
    return counts.reshape(N_ROW, N_COL).astype(jnp.int32)


def block_levels(stream_key, dims, pieces, smallest, largest):
    def one(axis_at, blocks):
        draws = jax.random.uniform(jax.random.fold_in(jax.random.fold_in(stream_key, 6), axis_at), (blocks,), jnp.float32, smallest / len(pieces), largest / len(pieces))
        return jnp.repeat(jnp.exp(draws), dims[axis_at] // blocks).reshape((-1,) + (1,) * (len(dims) - axis_at - 1))

    level = one(*pieces[0])
    for cut in pieces[1:]:
        level = level * one(*cut)
    return level


def noise(own_key, shape, width, most, cuts=(), held_as=jnp.bfloat16):
    array = jax.random.normal(own_key, shape, jnp.float32) * width
    if len(cuts) > 0:
        array = block_levels(own_key, shape, cuts, -0.22, 0.18) * array
    return jnp.clip(array, min=-most, max=most).astype(held_as)


def setup_inputs(seed: int = 0) -> dict:
    streams_of = jax.random.split(jax.random.key(seed), 8)
    features = noise(streams_of[0], (NV, F), 1.0, 6.0, ((0, 64), (1, 4)))
    weight = noise(streams_of[1], (F, F), F ** -0.5, 0.25)
    cotangent = noise(streams_of[2], (NV, F), 1.0, 6.0, ((0, 64), (1, 4)))
    adjacency_blocks = noise(streams_of[3], (N_ROW, N_COL, NB, BLOCK, BLOCK), (NB * BLOCK * N_COL // RBT) ** -0.5, 0.078125, ((0, 16), (1, 4)))
    block_rows = draw_block_rows(jax.random.fold_in(streams_of[7], 71), 0)
    block_cols = draw_block_cols(jax.random.fold_in(streams_of[7], 71), 0)
    tile_counts = draw_tile_counts(jax.random.fold_in(streams_of[7], 71), 0)
    return {"features": features, "weight": weight, "cotangent": cotangent, "adjacency_blocks": adjacency_blocks, "block_rows": block_rows, "block_cols": block_cols, "tile_counts": tile_counts}


def activate(values):
    return jax.nn.gelu(values, approximate=True)

def tile_forward(blocks, rows_of, cols_of, tile_count, source):
    usable = (jnp.arange(NB) < tile_count).astype(jnp.float32)
    picked = source[cols_of]
    products = jnp.einsum('nij,njf->nif', blocks.astype(jnp.float32), picked)
    placing = (rows_of[None, :] == jnp.arange(RBT)[:, None]).astype(jnp.float32) * usable[None, :]
    return jnp.einsum('rn,nif->rif', placing, products)

def tile_backward(blocks, rows_of, cols_of, tile_count, target):
    usable = (jnp.arange(NB) < tile_count).astype(jnp.float32)
    picked = target[rows_of]
    products = jnp.einsum('nij,nif->njf', blocks.astype(jnp.float32), picked)
    placing = (cols_of[None, :] == jnp.arange(CBT)[:, None]).astype(jnp.float32) * usable[None, :]
    return jnp.einsum('cn,njf->cjf', placing, products)

def reference(features, weight, cotangent, adjacency_blocks, block_rows, block_cols, tile_counts):
    shards = features.astype(jnp.float32).reshape(N_ROW, N_COL, BP, BLOCK, F)

    def row_tile(row_index):
        summed = jnp.zeros((RBT, BLOCK, F), jnp.float32)
        for col_index in range(N_COL):
            source = shards[:, col_index].reshape(CBT, BLOCK, F)
            summed = summed + tile_forward(adjacency_blocks[row_index, col_index], block_rows[row_index, col_index], block_cols[row_index, col_index], tile_counts[row_index, col_index], source)
        return summed
    aggregated = lax.map(row_tile, jnp.arange(N_ROW)).reshape(NV, F).astype(jnp.bfloat16)
    mixed = jnp.dot(aggregated, weight, preferred_element_type=jnp.float32)
    activated = activate(mixed).astype(jnp.bfloat16)
    _, pullback = jax.vjp(activate, mixed)
    grad_mixed = pullback(cotangent.astype(jnp.float32))[0].astype(jnp.bfloat16)
    grad_weight = jnp.dot(aggregated.T, grad_mixed, preferred_element_type=jnp.float32)
    grad_aggregated = jnp.dot(grad_mixed, weight.T, preferred_element_type=jnp.float32).astype(jnp.bfloat16)
    targets = grad_aggregated.astype(jnp.float32).reshape(N_ROW, RBT, BLOCK, F)

    def col_tile(col_index):

        def accumulate(summed, row_index):
            extra = tile_backward(adjacency_blocks[row_index, col_index], block_rows[row_index, col_index], block_cols[row_index, col_index], tile_counts[row_index, col_index], targets[row_index])
            rounded = lax.optimization_barrier(extra.astype(jnp.bfloat16)).astype(jnp.float32)
            return (summed + rounded, None)
        summed, _ = lax.scan(accumulate, jnp.zeros((CBT, BLOCK, F), jnp.float32), jnp.arange(N_ROW))
        return summed
    gathered = lax.map(col_tile, jnp.arange(N_COL)).reshape(N_COL, N_ROW, BP, BLOCK, F)
    grad_features = jnp.transpose(gathered, (1, 0, 2, 3, 4)).reshape(NV, F).astype(jnp.bfloat16)
    return (activated, grad_features, grad_weight)
```

```python
import functools

import jax
import jax.numpy as jnp
from jax import lax
from jax.experimental import pallas as pl
from jax.experimental.pallas import tpu as pltpu
from jax.sharding import PartitionSpec as P

BF = jnp.bfloat16
F32 = jnp.float32
K = 4
CH = 32
BS = 256
FS = 128
GC = 0.7978845608028654
NB = 80
PF, CF, KF, LF = 0, 80, 160, 240
PB, RB, KB, LB = 256, 336, 416, 496


def sorted_slots(major, minor, span, valid, groups):
    slots = major.shape[0]
    at = jnp.arange(slots)
    key = jnp.where(valid, major * span + minor, 4096 + at)
    rank = jnp.sum((key[None, :] < key[:, None]).astype(jnp.int32), axis=1)
    hit = (rank[None, :] == at[:, None]).astype(jnp.int32)
    perm = jnp.sum(hit * at[None, :], axis=1)
    minor_sorted = jnp.sum(hit * minor[None, :], axis=1)
    major_sorted = jnp.sum(hit * major[None, :], axis=1)
    before = jnp.concatenate([jnp.full((1,), -1, jnp.int32), major_sorted[:-1]])
    keep = (major_sorted == before).astype(jnp.int32)
    g = jnp.arange(groups)
    ends = jnp.sum((valid[None, :] & (major[None, :] <= g[:, None])).astype(jnp.int32), axis=1)
    used = jnp.any(valid[None, :] & (major[None, :] == g[:, None]), axis=1)
    last = jnp.where(used, ends - 1, -1)
    return [perm, minor_sorted, keep, last]


def kernel(
    idx, feat, weight, cot, adj_hbm,
    act_out, gf_out, gw_out,
    adj, gath, work, buf, part, yrecv, agg, cott, gmix, wt, actt,
    tgt, terms, xfl, xfr, xol, xor_, lines, zfd, zfu, fin,
    gw, gwy, gwx, gwxr, gwz, gwxa,
    adj_sem,
    zsu, zsd, zr, xsr, xsl, xrl, xrr, osr, osl, orl, orr,
    ys, yr, ds, dr, cs, cr, gs, gr, ts, tr,
    asr, asl, arl, arr, bsr, bsl, brl, brr, us, dns, ur, dnr,
    wys, wyr, wxs, wxr, wzs, wzr, vxs, vxr, vys, vyr,
):
    row = lax.axis_index("row")
    c = lax.axis_index("col")
    d = lax.axis_index("depth")
    x, z = row // 4, row % 4
    zh, core = d // 2, d % 2
    right = {"row": (x + 1) % 4 * 4 + z}
    left = {"row": (x + 3) % 4 * 4 + z}
    up = {"row": x * 4 + (z + 1) % 4}
    down = {"row": x * 4 + (z + 3) % 4}
    d_core = zh * 2 + (1 - core)
    d_far = (1 - zh) * 2 + core
    d_diag = (1 - zh) * 2 + (1 - core)
    to_core = {"depth": d_core}
    to_far = {"depth": d_far}
    xr1, xl1, xop = (x + 1) % 4, (x + 3) % 4, (x + 2) % 4

    def rcopy(src, dst, ssem, rsem, dev):
        return pltpu.make_async_remote_copy(
            src_ref=src, dst_ref=dst, send_sem=ssem, recv_sem=rsem,
            device_id=dev, device_id_type=pl.DeviceIdType.MESH,
        )

    def go(op, *args):
        copy = rcopy(*args)
        if op == "start":
            copy.start()
        elif op == "sent":
            copy.wait_send()
        else:
            copy.wait_recv()

    barrier = pltpu.get_barrier_semaphore()
    for o in range(1, 4):
        for dev in (
            {"row": (x + o) % 4 * 4 + z},
            {"row": x * 4 + (z + o) % 4},
            {"col": (c + o) % 4},
        ):
            pl.semaphore_signal(barrier, inc=1, device_id=dev, device_id_type=pl.DeviceIdType.MESH)
    for dev in (to_core, to_far):
        pl.semaphore_signal(barrier, inc=1, device_id=dev, device_id_type=pl.DeviceIdType.MESH)

    adj_copy = pltpu.make_async_copy(adj_hbm, adj, adj_sem)
    adj_copy.start()

    for b in range(4):
        flip = feat[b * BS:(b + 1) * BS, :].astype(F32).T.astype(BF)
        for k in range(K):
            gath[k, row * 4 + b] = flip[k * CH:(k + 1) * CH]

    pl.semaphore_wait(barrier, 11)

    def shard(k, xx, zz):
        return gath.at[k, pl.ds((xx * 4 + zz) * 4, 4)]

    def lower(k, xx, zz):
        return gath.at[k, pl.ds((xx * 4 + zz) * 4, 2)]

    def upper(k, xx, zz):
        return gath.at[k, pl.ds((xx * 4 + zz) * 4 + 2, 2)]

    def z_up(op, k, zz):
        go(op, shard(k, x, zz), shard(k, x, zz), zsu.at[k, zz], zr.at[k, zz], up)

    def z_down(op, k, zz):
        go(op, shard(k, x, zz), shard(k, x, zz), zsd.at[k, zz], zr.at[k, zz], down)

    def z_own(op, k):
        @pl.when(z < 3)
        def _():
            z_up(op, k, z)

        @pl.when(z > 0)
        def _():
            z_down(op, k, z)

    def x_send(op, k, zz):
        go(op, shard(k, x, zz), shard(k, x, zz), xsr.at[k, zz], xrl.at[k, zz], right)
        go(op, shard(k, x, zz), shard(k, x, zz), xsl.at[k, zz], xrr.at[k, zz], left)

    def z_stage(op, k):
        for o in range(1, 4):
            @pl.when(z >= o)
            def _():
                zz = z - o
                if op == "start":
                    z_up("recv", k, zz)

                @pl.when(z < 3)
                def _():
                    z_up(op, k, zz)
                x_send(op, k, zz)

            @pl.when(z + o <= 3)
            def _():
                zz = z + o
                if op == "start":
                    z_down("recv", k, zz)

                @pl.when(z > 0)
                def _():
                    z_down(op, k, zz)
                x_send(op, k, zz)

    def x_pass(op, k):
        def one(i, _):
            zz = (z + i) % 4
            if op == "start":
                go("recv", shard(k, xl1, zz), shard(k, xl1, zz), xsr.at[k, zz], xrl.at[k, zz], right)
            go(op, lower(k, xl1, zz), lower(k, xl1, zz), osr.at[k, zz], orl.at[k, zz], right)
            if op == "start":
                go("recv", shard(k, xr1, zz), shard(k, xr1, zz), xsl.at[k, zz], xrr.at[k, zz], left)
            go(op, upper(k, xr1, zz), upper(k, xr1, zz), osl.at[k, zz], orr.at[k, zz], left)
            return 0
        lax.fori_loop(0, 4, one, 0)

    def x_last(k):
        def one(i, _):
            zz = (z + i) % 4
            go("recv", lower(k, xop, zz), lower(k, xop, zz), osr.at[k, zz], orl.at[k, zz], right)
            go("recv", upper(k, xop, zz), upper(k, xop, zz), osl.at[k, zz], orr.at[k, zz], left)
            return 0
        lax.fori_loop(0, 4, one, 0)

    def y_send(op, k):
        for o in range(1, 4):
            to = (c + o) % 4
            go(op, part.at[k, pl.ds(to * 4, 4)], yrecv.at[k, c], ys.at[k, o], yr.at[k, c], {"col": to})

    def y_sum(k):
        for o in range(1, 4):
            src = (c + o) % 4
            go("recv", part.at[k, pl.ds(c * 4, 4)], yrecv.at[k, src], ys.at[k, o], yr.at[k, src], {"col": src})
        for b in range(4):
            total = part[k, c * 4 + b].astype(F32)
            for o in range(1, 4):
                total = total + yrecv[k, (c + o) % 4, b].astype(F32)
            agg[b, pl.ds(pl.multiple_of(d * FS + k * CH, CH), CH), :] = total.astype(BF)

    def agg_rows(dd, k):
        return agg.at[:, pl.ds(pl.multiple_of(dd * FS + k * CH, CH), CH), :]

    def d_send(op, k):
        go(op, agg_rows(d, k), agg_rows(d, k), ds.at[k, 1], dr.at[k, 1], to_far)
        go(op, agg_rows(d, k), agg_rows(d, k), ds.at[k, 0], dr.at[k, 0], to_core)

    def d_pass(op, k):
        if op == "start":
            go("recv", agg_rows(d_far, k), agg_rows(d_far, k), ds.at[k, 1], dr.at[k, 1], to_far)
        go(op, agg_rows(d_far, k), agg_rows(d_far, k), ds.at[k, 2], dr.at[k, 2], to_core)

    def d_last(k):
        go("recv", agg_rows(d_core, k), agg_rows(d_core, k), ds.at[k, 0], dr.at[k, 0], to_core)
        go("recv", agg_rows(d_diag, k), agg_rows(d_diag, k), ds.at[k, 2], dr.at[k, 2], to_core)

    def cot_send(op):
        go(op, cott.at[zh], cott.at[zh], cs.at[0], cr.at[0], to_far)

    def forward_tile(k):
        def move(i, _):
            work[i] = gath[k, i]
            return 0
        lax.fori_loop(0, 64, move, 0, unroll=4)

        def slot(s, acc):
            prod = lax.dot_general(
                work[idx[CF + s]], adj[idx[PF + s]], (((1,), (1,)), ((), ())),
                preferred_element_type=F32,
            )
            acc = acc * idx[KF + s].astype(F32) + prod
            buf[s] = acc.astype(BF)
            return acc
        lax.fori_loop(0, NB, slot, jnp.zeros((CH, BS), F32), unroll=8)

        def pick(i, _):
            last = idx[LF + i]
            on = (jnp.minimum(last, 0) + 1).astype(F32)
            part[k, i] = (buf[jnp.maximum(last, 0)].astype(F32) * on).astype(BF)
            return 0
        lax.fori_loop(0, 16, pick, 0, unroll=4)

    z_own("start", 0)
    x_send("start", 0, z)

    for b in range(4):
        cott[zh, b] = cot[b * BS:(b + 1) * BS, :].astype(F32).T.astype(BF)
    z_stage("start", 0)
    cot_send("start")
    for i in range(2):
        for j in range(4):
            cols = pl.ds(pl.multiple_of((i * 2 + core) * FS, FS), FS)
            wt[i, :, j * FS:(j + 1) * FS] = weight[j * FS:(j + 1) * FS, cols].astype(F32).T.astype(BF)
    adj_copy.wait()

    def forward_step(k, _):
        @pl.when(k + 1 < K)
        def _():
            z_own("start", k + 1)
        x_pass("start", k)

        @pl.when(k + 1 < K)
        def _():
            x_send("start", k + 1, z)
            z_stage("start", k + 1)
        x_last(k)
        forward_tile(k)
        y_send("start", k)

        @pl.when(k > 0)
        def _():
            y_sum(k - 1)
            d_send("start", k - 1)

        @pl.when(k > 1)
        def _():
            d_pass("start", k - 2)
        return 0
    lax.fori_loop(0, K, forward_step, 0)
    y_sum(K - 1)
    d_send("start", K - 1)
    d_pass("start", K - 2)
    d_pass("start", K - 1)
    go("recv", cott.at[1 - zh], cott.at[1 - zh], cs.at[0], cr.at[0], to_far)
    for k in range(K):
        d_last(k)

    def mix_rows(b, dd):
        return gmix.at[b, pl.ds(pl.multiple_of(dd * FS, FS), FS), :]

    def mix_send(op, b):
        go(op, mix_rows(b, d), mix_rows(b, d), gs.at[b, 0], gr.at[b, 0], to_core)
        go(op, mix_rows(b, d_far), mix_rows(b, d_far), gs.at[b, 1], gr.at[b, 1], to_core)

    def mix_last(b):
        go("recv", mix_rows(b, d_core), mix_rows(b, d_core), gs.at[b, 0], gr.at[b, 0], to_core)
        go("recv", mix_rows(b, d_diag), mix_rows(b, d_diag), gs.at[b, 1], gr.at[b, 1], to_core)

    def dense(b, _):
        for own in (True, False):
            at = zh if own else 1 - zh
            dd = at * 2 + core
            m = jnp.dot(wt[at], agg[b], preferred_element_type=F32)
            sq = m * m
            t = jnp.tanh(GC * (m + 0.044715 * (sq * m)))
            half = 0.5 + 0.5 * t
            if own:
                actt[b] = (m * half).astype(BF)
            slope = half + 0.5 * m * (1.0 - t * t) * (GC + (3 * 0.044715 * GC) * sq)
            gmix[b, pl.ds(pl.multiple_of(dd * FS, FS), FS), :] = (
                cott[at, b].astype(F32) * slope
            ).astype(BF)
        mix_send("start", b)
        return 0
    lax.fori_loop(0, 4, dense, 0)

    def back_mix(b, _):
        mix_last(b)
        ga = jnp.dot(
            weight[pl.ds(pl.multiple_of(d * FS, FS), FS), :], gmix[b], preferred_element_type=F32
        ).astype(BF)
        for k in range(K):
            tgt[k, c * 4 + b] = ga[k * CH:(k + 1) * CH]
        return 0
    lax.fori_loop(0, 4, back_mix, 0)

    def t_send(op, k):
        own = tgt.at[k, pl.ds(c * 4, 4)]
        for o in range(1, 4):
            go(op, own, own, ts.at[k, o], tr.at[k, c], {"col": (c + o) % 4})

    def t_last(k):
        for o in range(1, 4):
            src = (c + o) % 4
            ref = tgt.at[k, pl.ds(src * 4, 4)]
            go("recv", ref, ref, ts.at[k, o], tr.at[k, src], {"col": src})

    for k in range(K):
        t_send("start", k)

    def gw_block(b, _):
        own = agg[b, pl.ds(pl.multiple_of(d * FS, FS), FS), :]
        for j in range(2):
            add = lax.dot_general(
                own, gmix[b, j * 256:(j + 1) * 256, :], (((1,), (1,)), ((), ())),
                preferred_element_type=F32,
            )
            for q in range(4):
                gw[q, :, j * 256:(j + 1) * 256] += add[q * 32:(q + 1) * 32]
        return 0
    gw[...] = jnp.zeros_like(gw)
    lax.fori_loop(0, 4, gw_block, 0)

    def wy(op, o):
        to = (c + o) % 4
        go(op, gw.at[to], gwy.at[c], wys.at[o], wyr.at[c], {"col": to})

    def wx(op, o):
        to = (x + o) % 4
        go(op, gwx.at[to], gwxr.at[x], wxs.at[o], wxr.at[x], {"row": to * 4 + z})

    def wz(op, o):
        go(op, gwz.at[z], gwz.at[z], wzs.at[o], wzr.at[z], {"row": x * 4 + (z + o) % 4})

    def vx(op, o):
        go(op, gwxa.at[x], gwxa.at[x], vxs.at[o], vxr.at[x], {"row": (x + o) % 4 * 4 + z})

    def vy(op, o):
        own = gw_out.at[pl.ds(pl.multiple_of(c * 32, 32), 32), :]
        go(op, own, own, vys.at[o], vyr.at[c], {"col": (c + o) % 4})

    def all3(fn, op):
        for o in range(1, 4):
            fn(op, o)

    def weight_step(it):
        @pl.when(it == 1)
        def _():
            for o in range(1, 4):
                src = (c + o) % 4
                go("recv", gw.at[c], gwy.at[src], wys.at[o], wyr.at[src], {"col": src})
            total = gw[c]
            for o in range(1, 4):
                total = total + gwy[(c + o) % 4]
            for q in range(4):
                gwx[q] = total[q * 8:(q + 1) * 8]
            all3(wx, "start")

        @pl.when(it == 2)
        def _():
            for o in range(1, 4):
                src = (x + o) % 4
                go("recv", gwx.at[x], gwxr.at[src], wxs.at[o], wxr.at[src], right)
            total = gwx[x]
            for o in range(1, 4):
                total = total + gwxr[(x + o) % 4]
            gwz[z] = total
            all3(wz, "start")

        @pl.when(it == 3)
        def _():
            for o in range(1, 4):
                src = (z + o) % 4
                go("recv", gwz.at[src], gwz.at[src], wzs.at[o], wzr.at[src], up)
            gwxa[x] = (gwz[0] + gwz[1]) + (gwz[2] + gwz[3])
            all3(vx, "start")

        @pl.when(it == 4)
        def _():
            for o in range(1, 4):
                src = (x + o) % 4
                go("recv", gwxa.at[src], gwxa.at[src], vxs.at[o], vxr.at[src], right)
            for q in range(4):
                gw_out[pl.ds(pl.multiple_of(c * 32 + q * 8, 8), 8), :] = gwxa[q]
            all3(vy, "start")

    all3(wy, "start")

    for b in range(4):
        act_out[b * BS:(b + 1) * BS, :] = actt[b].astype(F32).T.astype(BF)

    def backward_tile(k):
        t_last(k)

        def move(i, _):
            work[i] = tgt[k, i]
            return 0
        lax.fori_loop(0, 16, move, 0, unroll=4)

        def slot(s, acc):
            prod = jnp.dot(work[idx[RB + s]], adj[idx[PB + s]], preferred_element_type=F32)
            acc = acc * idx[KB + s].astype(F32) + prod
            buf[s] = acc.astype(BF)
            return acc
        lax.fori_loop(0, NB, slot, jnp.zeros((CH, BS), F32), unroll=8)

        def pick(i, _):
            last = idx[LB + i]
            on = (jnp.minimum(last, 0) + 1).astype(F32)
            terms[k, i] = (buf[jnp.maximum(last, 0)].astype(F32) * on).astype(BF)
            return 0
        lax.fori_loop(0, 64, pick, 0, unroll=4)

    def term(k, xx, zz, n=4, lo=0):
        return terms.at[k, pl.ds((xx * 4 + zz) * 4 + lo, n)]

    def far_half(op, k):
        def one(i, _):
            zz = (z + i) % 4
            go(op, term(k, xop, zz, 2), xol.at[k, zz], asr.at[k, zz], arl.at[k, zz], right)
            go(op, term(k, xop, zz, 2, 2), xor_.at[k, zz], asl.at[k, zz], arr.at[k, zz], left)
            return 0
        lax.fori_loop(0, 4, one, 0)

    def near_full(op, k):
        def one(i, _):
            zz = (z + i) % 4
            if op == "start":
                go("recv", term(k, xop, zz, 2), xol.at[k, zz], asr.at[k, zz], arl.at[k, zz], right)
                at = (xr1 * 4 + zz) * 4
                for h in range(2):
                    terms[k, at + h] = (terms[k, at + h].astype(F32) + xol[k, zz, h].astype(F32)).astype(BF)
            go(op, term(k, xr1, zz), xfl.at[k, zz], bsr.at[k, zz], brl.at[k, zz], right)
            if op == "start":
                go("recv", term(k, xop, zz, 2, 2), xor_.at[k, zz], asl.at[k, zz], arr.at[k, zz], left)
                at = (xl1 * 4 + zz) * 4 + 2
                for h in range(2):
                    terms[k, at + h] = (terms[k, at + h].astype(F32) + xor_[k, zz, h].astype(F32)).astype(BF)
            go(op, term(k, xl1, zz), xfr.at[k, zz], bsl.at[k, zz], brr.at[k, zz], left)
            return 0
        lax.fori_loop(0, 4, one, 0)

    def x_sum(k):
        def one(i, _):
            zz = (z + i) % 4
            go("recv", term(k, xr1, zz), xfl.at[k, zz], bsr.at[k, zz], brl.at[k, zz], right)
            go("recv", term(k, xl1, zz), xfr.at[k, zz], bsl.at[k, zz], brr.at[k, zz], left)
            for b in range(4):
                lines[k, zz, b] = (
                    terms[k, (x * 4 + zz) * 4 + b].astype(F32)
                    + xfl[k, zz, b].astype(F32)
                    + xfr[k, zz, b].astype(F32)
                ).astype(BF)
            return 0
        lax.fori_loop(0, 4, one, 0)

    def line_up(op, k):
        for zz in (3, 2, 1):
            @pl.when(z < zz)
            def _():
                if op == "start":
                    @pl.when(z > 0)
                    def _():
                        go("recv", lines.at[k, zz], zfd.at[k, zz], us.at[k, zz], dnr.at[k, zz], up)
                        for b in range(4):
                            lines[k, zz, b] = (
                                lines[k, zz, b].astype(F32) + zfd[k, zz, b].astype(F32)
                            ).astype(BF)
                go(op, lines.at[k, zz], zfd.at[k, zz], us.at[k, zz], dnr.at[k, zz], up)

    def line_down(op, k):
        for zz in (0, 1, 2):
            @pl.when(z > zz)
            def _():
                if op == "start":
                    @pl.when(z < 3)
                    def _():
                        go("recv", lines.at[k, zz], zfu.at[k, zz], dns.at[k, zz], ur.at[k, zz], down)
                        for b in range(4):
                            lines[k, zz, b] = (
                                lines[k, zz, b].astype(F32) + zfu[k, zz, b].astype(F32)
                            ).astype(BF)
                go(op, lines.at[k, zz], zfu.at[k, zz], dns.at[k, zz], ur.at[k, zz], down)

    def finish(k):
        rows = pl.ds(pl.multiple_of(k * CH, CH), CH)
        for b in range(4):
            fin[b, rows, :] = lines[k, z, b].astype(F32)

        @pl.when(z > 0)
        def _():
            go("recv", lines.at[k, z], zfd.at[k, z], us.at[k, z], dnr.at[k, z], up)
            for b in range(4):
                fin[b, rows, :] += zfd[k, z, b].astype(F32)

        @pl.when(z < 3)
        def _():
            go("recv", lines.at[k, z], zfu.at[k, z], dns.at[k, z], ur.at[k, z], down)
            for b in range(4):
                fin[b, rows, :] += zfu[k, z, b].astype(F32)

    def backward_step(it, _):
        @pl.when(it < K)
        def _():
            backward_tile(it)
            far_half("start", it)

        @pl.when((it > 0) & (it <= K))
        def _():
            x_sum(it - 1)

        @pl.when(it < K)
        def _():
            near_full("start", it)
        ku = it - 1 - z

        @pl.when((ku >= 0) & (ku < K))
        def _():
            line_up("start", ku)
        kd = it - 4 + z

        @pl.when((kd >= 0) & (kd < K))
        def _():
            line_down("start", kd)

        @pl.when(it >= 4)
        def _():
            finish(it - 4)
        weight_step(it)
        return 0
    lax.fori_loop(0, K + 4, backward_step, 0)

    for b in range(4):
        gf_out[b * BS:(b + 1) * BS, :] = fin[b].T.astype(BF)
    for o in range(1, 4):
        src = (c + o) % 4
        ref = gw_out.at[pl.ds(pl.multiple_of(src * 32, 32), 32), :]
        go("recv", ref, ref, vys.at[o], vyr.at[src], {"col": src})

    def drain(k, _):
        z_own("sent", k)
        x_send("sent", k, z)
        z_stage("sent", k)
        x_pass("sent", k)
        y_send("sent", k)
        d_send("sent", k)
        d_pass("sent", k)
        mix_send("sent", k)
        t_send("sent", k)
        far_half("sent", k)
        near_full("sent", k)
        line_up("sent", k)
        line_down("sent", k)
        return 0
    lax.fori_loop(0, K, drain, 0)
    cot_send("sent")
    for fn in (wy, wx, wz, vx, vy):
        all3(fn, "sent")


def layer(features, weight, cotangent, adjacency_blocks, block_rows, block_cols, tile_counts):
    blocks = adjacency_blocks[0, 0]
    rows_of, cols_of, count = block_rows[0, 0], block_cols[0, 0], tile_counts[0, 0]
    valid = jnp.arange(NB) < count
    idx = jnp.concatenate(
        sorted_slots(rows_of, cols_of, 64, valid, 16) + sorted_slots(cols_of, rows_of, 16, valid, 64)
    )
    vm = pl.BlockSpec(memory_space=pltpu.VMEM)
    dma = lambda *s: pltpu.SemaphoreType.DMA(s)
    per_chunk = (K, 4)
    scratch = [
        pltpu.VMEM((NB, BS, BS), BF),
        pltpu.VMEM((K, 64, CH, BS), BF),
        pltpu.VMEM((64, CH, BS), BF),
        pltpu.VMEM((NB, CH, BS), BF),
        pltpu.VMEM((K, 16, CH, BS), BF),
        pltpu.VMEM((K, 4, 4, CH, BS), BF),
        pltpu.VMEM((4, 512, BS), BF),
        pltpu.VMEM((2, 4, FS, BS), BF),
        pltpu.VMEM((4, 512, BS), BF),
        pltpu.VMEM((2, FS, 512), BF),
        pltpu.VMEM((4, FS, BS), BF),
        pltpu.VMEM((K, 16, CH, BS), BF),
        pltpu.VMEM((K, 64, CH, BS), BF),
        pltpu.VMEM((K, 4, 4, CH, BS), BF),
        pltpu.VMEM((K, 4, 4, CH, BS), BF),
        pltpu.VMEM((K, 4, 2, CH, BS), BF),
        pltpu.VMEM((K, 4, 2, CH, BS), BF),
        pltpu.VMEM((K, 4, 4, CH, BS), BF),
        pltpu.VMEM((K, 4, 4, CH, BS), BF),
        pltpu.VMEM((K, 4, 4, CH, BS), BF),
        pltpu.VMEM((4, FS, BS), F32),
        pltpu.VMEM((4, 32, 512), F32),
        pltpu.VMEM((4, 32, 512), F32),
        pltpu.VMEM((4, 8, 512), F32),
        pltpu.VMEM((4, 8, 512), F32),
        pltpu.VMEM((4, 8, 512), F32),
        pltpu.VMEM((4, 8, 512), F32),
        pltpu.SemaphoreType.DMA,
    ]
    scratch += [dma(*per_chunk) for _ in range(11)]
    scratch += [dma(K, 4), dma(K, 4), dma(K, 3), dma(K, 3), dma(1), dma(1), dma(4, 2), dma(4, 2), dma(K, 4), dma(K, 4)]
    scratch += [dma(*per_chunk) for _ in range(12)]
    scratch += [dma(4) for _ in range(10)]
    return pl.pallas_call(
        kernel,
        out_shape=(
            jax.ShapeDtypeStruct(features.shape, BF),
            jax.ShapeDtypeStruct(features.shape, BF),
            jax.ShapeDtypeStruct((FS, 512), F32),
        ),
        in_specs=[pl.BlockSpec(memory_space=pltpu.SMEM), vm, vm, vm, pl.BlockSpec(memory_space=pl.ANY)],
        out_specs=(vm, vm, vm),
        scratch_shapes=scratch,
        compiler_params=pltpu.CompilerParams(
            collective_id=0, has_side_effects=True, vmem_limit_bytes=56 << 20
        ),
        cost_estimate=pl.CostEstimate(flops=4_000_000_000, bytes_accessed=13_000_000, transcendentals=300_000),
    )(idx, features, weight, cotangent, blocks)


def solution(mesh):
    in_specs = (
        P(("row", "col"), "depth"),
        P(),
        P(("row", "col"), "depth"),
        P("row", "col", None, None, None),
        P("row", "col", None),
        P("row", "col", None),
        P("row", "col"),
    )
    out_specs = (P(("row", "col"), "depth"), P(("row", "col"), "depth"), P("depth", None))
    return jax.shard_map(layer, mesh=mesh, in_specs=in_specs, out_specs=out_specs, check_vma=False)
```

```python
import jax
import jax.numpy as jnp
from jax import lax
from jax.experimental import pallas as pl
from jax.experimental.pallas import tpu as pltpu
from jax.sharding import PartitionSpec as P

BF = jnp.bfloat16
F32 = jnp.float32
K = 2
CH = 64
BS = 256
PB = 1
NP = 4 // PB
FS = 128
GC = 0.7978845608028654
NB = 80
PF, CF, KF, LF, QB, RB, KB, LB = range(8)


def slot_order(major, minor, span, valid):
    side = major.shape[0]
    lane = lax.broadcasted_iota(jnp.int32, (side, side), 1)
    key = jnp.where(valid, major * span + minor, 4096 + lane)
    key_t, major_t, minor_t = key.T, major.T, minor.T
    valid_t = valid.astype(jnp.int32).T > 0
    rank = jnp.sum((key < key_t).astype(jnp.int32), axis=1, keepdims=True)
    at = lax.broadcasted_iota(jnp.int32, (side, side), 0)

    def pick(cond, value):
        return jnp.sum(jnp.where(cond, value, 0), axis=0, keepdims=True)

    hit = rank == lane
    perm = pick(hit, at)
    minor_sorted = pick(hit, minor_t)
    major_sorted = pick(hit, major_t + 1)
    before = pick(rank + 1 == lane, major_t + 1)
    keep = (major_sorted == before).astype(jnp.int32)
    ends = pick(valid_t & (major_t <= lane), 1)
    used = pick(valid_t & (major_t == lane), 1)
    last = jnp.where(used > 0, ends - 1, -1)
    return [perm, minor_sorted, keep, last]


def kernel(
    count, rows_of, cols_of, feat, weight, cot, adj_hbm,
    act_out, gf_out, gw_out,
    idx, table, idx_sem,
    adj, gath, work, buf, part, yrecv, agg, cott, gmix, wt,
    tgt, terms, xfl, xfr, xol, xor_, lines, zfd, zfu, z3d, z3u, xo3, xf3,
    gw, gwy, gwx, gwxr, gwz, gwxa,
    adj_sem,
    zsu, zsd, zr, xsr, xsl, xrl, xrr, osr, osl, orl, orr,
    ys, yr, ds, dr, cs, cr, gs, gr, ts, tr,
    asr, asl, arl, arr, bsr, bsl, brl, brr, us, dns, ur, dnr,
    u3s, d3s, u3r, d3r, o3s, o3r, f3s, f3r,
    wys, wyr, wxs, wxr, wzs, wzr, vxs, vxr, vys, vyr,
):
    row = lax.axis_index("row")
    c = lax.axis_index("col")
    d = lax.axis_index("depth")
    x, z = row // 4, row % 4
    zh, core = d // 2, d % 2
    right = {"row": (x + 1) % 4 * 4 + z}
    left = {"row": (x + 3) % 4 * 4 + z}
    up = {"row": x * 4 + (z + 1) % 4}
    down = {"row": x * 4 + (z + 3) % 4}
    d_core = zh * 2 + (1 - core)
    d_far = (1 - zh) * 2 + core
    d_diag = (1 - zh) * 2 + (1 - core)
    to_core = {"depth": d_core}
    to_far = {"depth": d_far}
    xr1, xl1, xop = (x + 1) % 4, (x + 3) % 4, (x + 2) % 4

    def rcopy(src, dst, ssem, rsem, dev):
        return pltpu.make_async_remote_copy(
            src_ref=src, dst_ref=dst, send_sem=ssem, recv_sem=rsem,
            device_id=dev, device_id_type=pl.DeviceIdType.MESH,
        )

    def go(op, *args):
        copy = rcopy(*args)
        if op == "start":
            copy.start()
        elif op == "sent":
            copy.wait_send()
        else:
            copy.wait_recv()

    barrier = pltpu.get_barrier_semaphore()
    for o in range(1, 4):
        for dev in (
            {"row": (x + o) % 4 * 4 + z},
            {"row": x * 4 + (z + o) % 4},
            {"col": (c + o) % 4},
        ):
            pl.semaphore_signal(barrier, inc=1, device_id=dev, device_id_type=pl.DeviceIdType.MESH)
    for dev in (to_core, to_far):
        pl.semaphore_signal(barrier, inc=1, device_id=dev, device_id_type=pl.DeviceIdType.MESH)

    adj_copy = pltpu.make_async_copy(adj_hbm, adj, adj_sem)
    adj_copy.start()

    for b in range(4):
        flip = feat[b * BS:(b + 1) * BS, :].astype(F32).T.astype(BF)
        for k in range(K):
            gath[k, row * 4 + b] = flip[k * CH:(k + 1) * CH]

    pl.semaphore_wait(barrier, 11)

    def shard(k, xx, zz):
        return gath.at[k, pl.ds((xx * 4 + zz) * 4, 4)]

    def lower(k, xx, zz):
        return gath.at[k, pl.ds((xx * 4 + zz) * 4, 2)]

    def upper(k, xx, zz):
        return gath.at[k, pl.ds((xx * 4 + zz) * 4 + 2, 2)]

    def z_up(op, k, zz):
        go(op, shard(k, x, zz), shard(k, x, zz), zsu.at[k, zz], zr.at[k, zz], up)

    def z_down(op, k, zz):
        go(op, shard(k, x, zz), shard(k, x, zz), zsd.at[k, zz], zr.at[k, zz], down)

    def z_own(op, k):
        @pl.when(z < 3)
        def _():
            z_up(op, k, z)

        @pl.when(z > 0)
        def _():
            z_down(op, k, z)

    def x_send(op, k, zz):
        go(op, shard(k, x, zz), shard(k, x, zz), xsr.at[k, zz], xrl.at[k, zz], right)
        go(op, shard(k, x, zz), shard(k, x, zz), xsl.at[k, zz], xrr.at[k, zz], left)

    def z_stage(op, k):
        for o in range(1, 4):
            @pl.when(z >= o)
            def _():
                zz = z - o
                if op == "start":
                    z_up("recv", k, zz)

                @pl.when(z < 3)
                def _():
                    z_up(op, k, zz)
                x_send(op, k, zz)

            @pl.when(z + o <= 3)
            def _():
                zz = z + o
                if op == "start":
                    z_down("recv", k, zz)

                @pl.when(z > 0)
                def _():
                    z_down(op, k, zz)
                x_send(op, k, zz)

    def x_pass(op, k):
        def one(i, _):
            zz = (z + i) % 4
            if op == "start":
                go("recv", shard(k, xl1, zz), shard(k, xl1, zz), xsr.at[k, zz], xrl.at[k, zz], right)
            go(op, lower(k, xl1, zz), lower(k, xl1, zz), osr.at[k, zz], orl.at[k, zz], right)
            if op == "start":
                go("recv", shard(k, xr1, zz), shard(k, xr1, zz), xsl.at[k, zz], xrr.at[k, zz], left)
            go(op, upper(k, xr1, zz), upper(k, xr1, zz), osl.at[k, zz], orr.at[k, zz], left)
            return 0
        lax.fori_loop(0, 4, one, 0)

    def x_last(k):
        def one(i, _):
            zz = (z + i) % 4
            go("recv", lower(k, xop, zz), lower(k, xop, zz), osr.at[k, zz], orl.at[k, zz], right)
            go("recv", upper(k, xop, zz), upper(k, xop, zz), osl.at[k, zz], orr.at[k, zz], left)
            return 0
        lax.fori_loop(0, 4, one, 0)

    def y_send(op, k, p):
        for o in range(1, 4):
            to = (c + o) % 4
            go(
                op, part.at[k, pl.ds(to * 4 + p * PB, PB)], yrecv.at[k, c, pl.ds(p * PB, PB)],
                ys.at[k, p, o], yr.at[k, p, c], {"col": to},
            )

    def y_sum(k, p):
        for o in range(1, 4):
            src = (c + o) % 4
            go(
                "recv", part.at[k, pl.ds(c * 4 + p * PB, PB)], yrecv.at[k, src, pl.ds(p * PB, PB)],
                ys.at[k, p, o], yr.at[k, p, src], {"col": src},
            )
        for q in range(PB):
            b = p * PB + q
            total = part[k, c * 4 + b].astype(F32)
            for o in range(1, 4):
                total = total + yrecv[k, (c + o) % 4, b].astype(F32)
            agg[b, pl.ds(pl.multiple_of(d * FS + k * CH, CH), CH), :] = total.astype(BF)

    def agg_rows(dd, k, p):
        return agg.at[pl.ds(p * PB, PB), pl.ds(pl.multiple_of(dd * FS + k * CH, CH), CH), :]

    def d_send(op, k, p):
        own = agg_rows(d, k, p)
        go(op, own, own, ds.at[k, p, 1], dr.at[k, p, 1], to_far)
        go(op, own, own, ds.at[k, p, 0], dr.at[k, p, 0], to_core)

    def d_pass(op, k, p):
        far = agg_rows(d_far, k, p)
        if op == "start":
            go("recv", far, far, ds.at[k, p, 1], dr.at[k, p, 1], to_far)
        go(op, far, far, ds.at[k, p, 2], dr.at[k, p, 2], to_core)

    def d_last(k, p):
        near, diag = agg_rows(d_core, k, p), agg_rows(d_diag, k, p)
        go("recv", near, near, ds.at[k, p, 0], dr.at[k, p, 0], to_core)
        go("recv", diag, diag, ds.at[k, p, 2], dr.at[k, p, 2], to_core)

    def blocks(fn, *args):
        def one(p, _):
            fn(*args, p)
            return 0
        lax.fori_loop(0, NP, one, 0)

    def cot_send(op):
        go(op, cott.at[zh], cott.at[zh], cs.at[0], cr.at[0], to_far)

    def forward_tile(k):
        def move(i, _):
            work[i] = gath[k, i]
            return 0
        lax.fori_loop(0, 64, move, 0, unroll=4)

        def slot(s, acc):
            prod = lax.dot_general(
                work[idx[CF, s]], adj[idx[PF, s]], (((1,), (1,)), ((), ())),
                preferred_element_type=F32,
            )
            acc = acc * idx[KF, s].astype(F32) + prod
            buf[s] = acc.astype(BF)
            return acc
        lax.fori_loop(0, NB, slot, jnp.zeros((CH, BS), F32), unroll=8)

        def pick(p, _):
            for q in range(4):
                for e in range(PB):
                    i = q * 4 + p * PB + e
                    last = idx[LF, i]
                    on = (jnp.minimum(last, 0) + 1).astype(F32)
                    part[k, i] = (buf[jnp.maximum(last, 0)].astype(F32) * on).astype(BF)
            y_send("start", k, p)
            return 0
        lax.fori_loop(0, NP, pick, 0)

    for k in range(min(2, K)):
        z_own("start", k)
        x_send("start", k, z)

    table[0:2, :] = jnp.zeros((2, 128), jnp.int32)
    table[0:1, 0:NB] = rows_of[...]
    table[1:2, 0:NB] = cols_of[...]
    rows_all = jnp.broadcast_to(table[0:1, :], (128, 128))
    cols_all = jnp.broadcast_to(table[1:2, :], (128, 128))
    valid = lax.broadcasted_iota(jnp.int32, (128, 128), 1) < count[0, 0]
    order = slot_order(rows_all, cols_all, 64, valid) + slot_order(cols_all, rows_all, 16, valid)
    for i in range(8):
        table[i:i + 1, :] = order[i]
    idx_copy = pltpu.make_async_copy(table, idx, idx_sem)
    idx_copy.start()

    z_stage("start", 0)
    for b in range(4):
        cott[zh, b] = cot[b * BS:(b + 1) * BS, :].astype(F32).T.astype(BF)
    if K > 1:
        z_stage("start", 1)
    if K == 2:
        cot_send("start")
    for i in range(2):
        for j in range(4):
            cols = pl.ds(pl.multiple_of((i * 2 + core) * FS, FS), FS)
            wt[i, :, j * FS:(j + 1) * FS] = weight[j * FS:(j + 1) * FS, cols].astype(F32).T.astype(BF)
    x_pass("start", 0)
    idx_copy.wait()
    adj_copy.wait()

    def forward_step(k, _):
        @pl.when(k + 2 < K)
        def _():
            z_own("start", k + 2)
            x_send("start", k + 2, z)
            z_stage("start", k + 2)

        @pl.when(k + 3 == K)
        def _():
            cot_send("start")

        @pl.when(k + 1 < K)
        def _():
            x_pass("start", k + 1)

        @pl.when(k > 0)
        def _():
            def one(p, _):
                y_sum(k - 1, p)
                d_send("start", k - 1, p)
                return 0
            lax.fori_loop(0, NP, one, 0)
        x_last(k)

        forward_tile(k)

        @pl.when(k > 0)
        def _():
            blocks(d_pass, "start", k - 1)
        return 0
    lax.fori_loop(0, K, forward_step, 0)

    def last_sum(p, _):
        y_sum(K - 1, p)
        d_send("start", K - 1, p)
        return 0
    lax.fori_loop(0, NP, last_sum, 0)
    go("recv", cott.at[1 - zh], cott.at[1 - zh], cs.at[0], cr.at[0], to_far)

    def mix_rows(p, dd):
        return gmix.at[pl.ds(p * PB, PB), pl.ds(pl.multiple_of(dd * FS, FS), FS), :]

    def mix_send(op, p):
        go(op, mix_rows(p, d), mix_rows(p, d), gs.at[p, 0], gr.at[p, 0], to_core)
        go(op, mix_rows(p, d_far), mix_rows(p, d_far), gs.at[p, 1], gr.at[p, 1], to_core)

    def mix_last(p):
        go("recv", mix_rows(p, d_core), mix_rows(p, d_core), gs.at[p, 0], gr.at[p, 0], to_core)
        go("recv", mix_rows(p, d_diag), mix_rows(p, d_diag), gs.at[p, 1], gr.at[p, 1], to_core)

    def dense(b):
        for own in (True, False):
            at = zh if own else 1 - zh
            dd = at * 2 + core
            m = jnp.dot(wt[at], agg[b], preferred_element_type=F32)
            sq = m * m
            t = jnp.tanh(GC * (m + 0.044715 * (sq * m)))
            half = 0.5 + 0.5 * t
            if own:
                act_out[b] = (m * half).astype(BF)
            slope = half + 0.5 * m * (1.0 - t * t) * (GC + (3 * 0.044715 * GC) * sq)
            gmix[b, pl.ds(pl.multiple_of(dd * FS, FS), FS), :] = (
                cott[at, b].astype(F32) * slope
            ).astype(BF)

    def back_mix(p):
        mix_last(p)

        def one(q, _):
            b = p * PB + q
            ga = jnp.dot(
                weight[pl.ds(pl.multiple_of(d * FS, FS), FS), :], gmix[b], preferred_element_type=F32
            ).astype(BF)
            for k in range(K):
                tgt[k, c * 4 + b] = ga[k * CH:(k + 1) * CH]
            return 0
        lax.fori_loop(0, PB, one, 0)
        t_send("start", 0, p)

    def t_send(op, k, p):
        own = tgt.at[k, pl.ds(c * 4 + p * PB, PB)]
        for o in range(1, 4):
            go(op, own, own, ts.at[k, p, o], tr.at[k, p, c], {"col": (c + o) % 4})

    def t_last(k):
        def one(p, _):
            for o in range(1, 4):
                src = (c + o) % 4
                ref = tgt.at[k, pl.ds(src * 4 + p * PB, PB)]
                go("recv", ref, ref, ts.at[k, p, o], tr.at[k, p, src], {"col": src})
            return 0
        lax.fori_loop(0, NP, one, 0)

    d_pass("start", K - 1, 0)

    def middle(p, _):
        @pl.when(p < NP - 1)
        def _():
            d_pass("start", K - 1, p + 1)
        for k in range(K):
            d_last(k, p)

        def one(q, _):
            dense(p * PB + q)
            return 0
        lax.fori_loop(0, PB, one, 0)
        mix_send("start", p)

        @pl.when(p > 0)
        def _():
            back_mix(p - 1)
        return 0
    lax.fori_loop(0, NP, middle, 0)
    back_mix(NP - 1)
    for k in range(1, K):
        blocks(t_send, "start", k)

    def gw_block(b, _):
        own = agg[b, pl.ds(pl.multiple_of(d * FS, FS), FS), :]
        for j in range(2):
            add = lax.dot_general(
                own, gmix[b, j * 256:(j + 1) * 256, :], (((1,), (1,)), ((), ())),
                preferred_element_type=F32,
            )
            for q in range(4):
                gw[q, :, j * 256:(j + 1) * 256] += add[q * 32:(q + 1) * 32]
        return 0
    gw[...] = jnp.zeros_like(gw)
    lax.fori_loop(0, 4, gw_block, 0)

    def wy(op, o):
        to = (c + o) % 4
        go(op, gw.at[to], gwy.at[c], wys.at[o], wyr.at[c], {"col": to})

    def wx(op, o):
        to = (x + o) % 4
        go(op, gwx.at[to], gwxr.at[x], wxs.at[o], wxr.at[x], {"row": to * 4 + z})

    def wz(op, o):
        go(op, gwz.at[z], gwz.at[z], wzs.at[o], wzr.at[z], {"row": x * 4 + (z + o) % 4})

    def vx(op, o):
        go(op, gwxa.at[x], gwxa.at[x], vxs.at[o], vxr.at[x], {"row": (x + o) % 4 * 4 + z})

    def vy(op, o):
        own = gw_out.at[pl.ds(pl.multiple_of(c * 32, 32), 32), :]
        go(op, own, own, vys.at[o], vyr.at[c], {"col": (c + o) % 4})

    def all3(fn, op):
        for o in range(1, 4):
            fn(op, o)

    def weight_step(it):
        if it == 1:
            for o in range(1, 4):
                src = (c + o) % 4
                go("recv", gw.at[c], gwy.at[src], wys.at[o], wyr.at[src], {"col": src})
            total = gw[c]
            for o in range(1, 4):
                total = total + gwy[(c + o) % 4]
            for q in range(4):
                gwx[q] = total[q * 8:(q + 1) * 8]
            all3(wx, "start")

        if it == 2:
            for o in range(1, 4):
                src = (x + o) % 4
                go("recv", gwx.at[x], gwxr.at[src], wxs.at[o], wxr.at[src], right)
            total = gwx[x]
            for o in range(1, 4):
                total = total + gwxr[(x + o) % 4]
            gwz[z] = total
            all3(wz, "start")

        if it == 3:
            for o in range(1, 4):
                src = (z + o) % 4
                go("recv", gwz.at[src], gwz.at[src], wzs.at[o], wzr.at[src], up)
            gwxa[x] = (gwz[0] + gwz[1]) + (gwz[2] + gwz[3])
            all3(vx, "start")

        if it == 4:
            for o in range(1, 4):
                src = (x + o) % 4
                go("recv", gwxa.at[src], gwxa.at[src], vxs.at[o], vxr.at[src], right)
            for q in range(4):
                gw_out[pl.ds(pl.multiple_of(c * 32 + q * 8, 8), 8), :] = gwxa[q]
            all3(vy, "start")

    all3(wy, "start")

    def backward_tile(k):
        t_last(k)

        def move(i, _):
            work[i] = tgt[k, i]
            return 0
        lax.fori_loop(0, 16, move, 0, unroll=4)

        def slot(s, acc):
            prod = jnp.dot(work[idx[RB, s]], adj[idx[QB, s]], preferred_element_type=F32)
            acc = acc * idx[KB, s].astype(F32) + prod
            buf[s] = acc.astype(BF)
            return acc
        lax.fori_loop(0, NB, slot, jnp.zeros((CH, BS), F32), unroll=8)

        def pick(i, _):
            last = idx[LB, i]
            on = (jnp.minimum(last, 0) + 1).astype(F32)
            terms[k, i // 16, i // 4 % 4, i % 4] = (buf[jnp.maximum(last, 0)].astype(F32) * on).astype(BF)
            return 0
        lax.fori_loop(0, 64, pick, 0, unroll=4)

    HALF = CH // 2
    order = (3, 0, 2, 1)

    def add_to(ref, at, got):
        ref[at] = (ref[at].astype(F32) + got.astype(F32)).astype(BF)

    def term(k, xx, zz, lo=0, n=CH):
        return terms.at[k, xx, zz, pl.ds(0, 3), pl.ds(lo, n)]

    def far_half(op, k):
        for zz in order:
            go(op, term(k, xop, zz, 0, HALF), xol.at[k, zz], asr.at[k, zz], arl.at[k, zz], right)
            go(op, term(k, xop, zz, HALF, HALF), xor_.at[k, zz], asl.at[k, zz], arr.at[k, zz], left)

    def near_full(op, k):
        for zz in order:
            if op == "start":
                go("recv", term(k, xop, zz, 0, HALF), xol.at[k, zz], asr.at[k, zz], arl.at[k, zz], right)
                for b in range(3):
                    add_to(terms, (k, xr1, zz, b, slice(0, HALF)), xol[k, zz, b])
            go(op, term(k, xr1, zz), xfl.at[k, zz], bsr.at[k, zz], brl.at[k, zz], right)
            if op == "start":
                go("recv", term(k, xop, zz, HALF, HALF), xor_.at[k, zz], asl.at[k, zz], arr.at[k, zz], left)
                for b in range(3):
                    add_to(terms, (k, xl1, zz, b, slice(HALF, CH)), xor_[k, zz, b])
            go(op, term(k, xl1, zz), xfr.at[k, zz], bsl.at[k, zz], brr.at[k, zz], left)

    def x_sum(k):
        for zz in order:
            go("recv", term(k, xr1, zz), xfl.at[k, zz], bsr.at[k, zz], brl.at[k, zz], right)
            go("recv", term(k, xl1, zz), xfr.at[k, zz], bsl.at[k, zz], brr.at[k, zz], left)
            for b in range(3):
                lines[k, zz, b] = (
                    terms[k, x, zz, b].astype(F32) + xfl[k, zz, b].astype(F32) + xfr[k, zz, b].astype(F32)
                ).astype(BF)
            if zz > 0:
                @pl.when(z == 0)
                def _():
                    up_msg("start", k, zz)
            if zz < 3:
                @pl.when(z == 3)
                def _():
                    down_msg("start", k, zz)

    def up_msg(op, k, zz):
        go(op, lines.at[k, zz], zfd.at[k, zz], us.at[k, zz], dnr.at[k, zz], up)

    def down_msg(op, k, zz):
        go(op, lines.at[k, zz], zfu.at[k, zz], dns.at[k, zz], ur.at[k, zz], down)

    def pass_on(op, k):
        for at, zz in ((1, 3), (1, 2), (2, 3)):
            @pl.when(z == at)
            def _():
                if op == "start":
                    up_msg("recv", k, zz)
                    for b in range(3):
                        add_to(lines, (k, zz, b), zfd[k, zz, b])
                up_msg(op, k, zz)

            @pl.when(z == 3 - at)
            def _():
                if op == "start":
                    down_msg("recv", k, 3 - zz)
                    for b in range(3):
                        add_to(lines, (k, 3 - zz, b), zfu[k, 3 - zz, b])
                down_msg(op, k, 3 - zz)

    def x_sum_sent(k):
        for zz in (1, 2, 3):
            @pl.when(z == 0)
            def _():
                up_msg("sent", k, zz)

            @pl.when(z == 3)
            def _():
                down_msg("sent", k, 3 - zz)

    def finish(k):
        rows = pl.ds(k * CH, CH)
        for b in range(3):
            gf_out[b, rows, :] = lines[k, z, b].astype(F32)

        @pl.when(z > 0)
        def _():
            up_msg("recv", k, z)
            for b in range(3):
                gf_out[b, rows, :] += zfd[k, z, b].astype(F32)

        @pl.when(z < 3)
        def _():
            down_msg("recv", k, z)
            for b in range(3):
                gf_out[b, rows, :] += zfu[k, z, b].astype(F32)

    def up3(op, k, zz):
        go(op, terms.at[k, :, zz, 3], z3d.at[k, zz], u3s.at[k, zz], d3r.at[k, zz], up)

    def down3(op, k, zz):
        go(op, terms.at[k, :, zz, 3], z3u.at[k, zz], d3s.at[k, zz], u3r.at[k, zz], down)

    def line3(op, k, stage):
        for zz in range(3, stage, -1):
            @pl.when(z == stage)
            def _():
                if op == "start" and stage > 0:
                    up3("recv", k, zz)
                    for q in range(4):
                        add_to(terms, (k, q, zz, 3), z3d[k, zz, q])
                up3(op, k, zz)

            @pl.when(z == 3 - stage)
            def _():
                if op == "start" and stage > 0:
                    down3("recv", k, 3 - zz)
                    for q in range(4):
                        add_to(terms, (k, q, 3 - zz, 3), z3u[k, 3 - zz, q])
                down3(op, k, 3 - zz)

    def line3_sum(k):
        @pl.when(z > 0)
        def _():
            up3("recv", k, z)
            for q in range(4):
                add_to(terms, (k, q, z, 3), z3d[k, z, q])

        @pl.when(z < 3)
        def _():
            down3("recv", k, z)
            for q in range(4):
                add_to(terms, (k, q, z, 3), z3u[k, z, q])

    def one3(k, xx, lo=0, n=CH):
        return terms.at[k, xx, z, 3, pl.ds(lo, n)]

    def far3(op, k):
        go(op, one3(k, xop, 0, HALF), xo3.at[k, 0], o3s.at[k, 0], o3r.at[k, 0], right)
        go(op, one3(k, xop, HALF, HALF), xo3.at[k, 1], o3s.at[k, 1], o3r.at[k, 1], left)

    def near3(op, k):
        if op == "start":
            go("recv", one3(k, xop, 0, HALF), xo3.at[k, 0], o3s.at[k, 0], o3r.at[k, 0], right)
            add_to(terms, (k, xr1, z, 3, slice(0, HALF)), xo3[k, 0])
        go(op, one3(k, xr1), xf3.at[k, 0], f3s.at[k, 0], f3r.at[k, 0], right)
        if op == "start":
            go("recv", one3(k, xop, HALF, HALF), xo3.at[k, 1], o3s.at[k, 1], o3r.at[k, 1], left)
            add_to(terms, (k, xl1, z, 3, slice(HALF, CH)), xo3[k, 1])
        go(op, one3(k, xl1), xf3.at[k, 1], f3s.at[k, 1], f3r.at[k, 1], left)

    def finish3(k):
        go("recv", one3(k, xr1), xf3.at[k, 0], f3s.at[k, 0], f3r.at[k, 0], right)
        go("recv", one3(k, xl1), xf3.at[k, 1], f3s.at[k, 1], f3r.at[k, 1], left)
        gf_out[3, k * CH:(k + 1) * CH, :] = (
            terms[k, x, z, 3].astype(F32) + xf3[k, 0].astype(F32) + xf3[k, 1].astype(F32)
        )

    backward_tile(0)
    far_half("start", 0)
    line3("start", 0, 0)
    backward_tile(1)
    line3("start", 1, 0)
    line3("start", 0, 1)
    near_full("start", 0)
    far_half("start", 1)
    line3("start", 0, 2)
    weight_step(1)
    line3("start", 1, 1)
    line3_sum(0)
    far3("start", 0)
    line3("start", 1, 2)
    x_sum(0)
    near_full("start", 1)
    near3("start", 0)
    line3_sum(1)
    far3("start", 1)
    weight_step(2)
    pass_on("start", 0)
    near3("start", 1)
    finish3(0)
    weight_step(3)
    finish(0)
    finish3(1)
    weight_step(4)
    x_sum(1)
    pass_on("start", 1)
    finish(1)

    for o in range(1, 4):
        src = (c + o) % 4
        ref = gw_out.at[pl.ds(pl.multiple_of(src * 32, 32), 32), :]
        go("recv", ref, ref, vys.at[o], vyr.at[src], {"col": src})

    def drain(k, _):
        z_own("sent", k)
        x_send("sent", k, z)
        z_stage("sent", k)
        x_pass("sent", k)
        for fn in (y_send, d_send, d_pass, t_send):
            blocks(fn, "sent", k)
        far_half("sent", k)
        near_full("sent", k)
        x_sum_sent(k)
        pass_on("sent", k)
        for stage in range(3):
            line3("sent", k, stage)
        far3("sent", k)
        near3("sent", k)
        return 0
    lax.fori_loop(0, K, drain, 0)
    blocks(mix_send, "sent")
    cot_send("sent")
    for fn in (wy, wx, wz, vx, vy):
        all3(fn, "sent")


def write_out(act_t, gf_t, gw, act, gf, gw_out):
    gw_out[...] = gw[...]
    for b in range(4):
        act[b * BS:(b + 1) * BS, :] = act_t[b].astype(F32).T.astype(BF)
        gf[b * BS:(b + 1) * BS, :] = gf_t[b].T.astype(BF)


def layer(features, weight, cotangent, adjacency_blocks, block_rows, block_cols, tile_counts):
    blocks = adjacency_blocks[0, 0]
    vm = pl.BlockSpec(memory_space=pltpu.VMEM)
    dma = lambda *s: pltpu.SemaphoreType.DMA(s)
    per_chunk = (K, 4)
    scratch = [
        pltpu.SMEM((8, 128), jnp.int32),
        pltpu.VMEM((8, 128), jnp.int32),
        pltpu.SemaphoreType.DMA,
        pltpu.VMEM((NB, BS, BS), BF),
        pltpu.VMEM((K, 64, CH, BS), BF),
        pltpu.VMEM((64, CH, BS), BF),
        pltpu.VMEM((NB, CH, BS), BF),
        pltpu.VMEM((K, 16, CH, BS), BF),
        pltpu.VMEM((K, 4, 4, CH, BS), BF),
        pltpu.VMEM((4, 512, BS), BF),
        pltpu.VMEM((2, 4, FS, BS), BF),
        pltpu.VMEM((4, 512, BS), BF),
        pltpu.VMEM((2, FS, 512), BF),
        pltpu.VMEM((K, 16, CH, BS), BF),
        pltpu.VMEM((K, 4, 4, 4, CH, BS), BF),
        pltpu.VMEM((K, 4, 3, CH, BS), BF),
        pltpu.VMEM((K, 4, 3, CH, BS), BF),
        pltpu.VMEM((K, 4, 3, CH // 2, BS), BF),
        pltpu.VMEM((K, 4, 3, CH // 2, BS), BF),
        pltpu.VMEM((K, 4, 3, CH, BS), BF),
        pltpu.VMEM((K, 4, 3, CH, BS), BF),
        pltpu.VMEM((K, 4, 3, CH, BS), BF),
        pltpu.VMEM((K, 4, 4, CH, BS), BF),
        pltpu.VMEM((K, 4, 4, CH, BS), BF),
        pltpu.VMEM((K, 2, CH // 2, BS), BF),
        pltpu.VMEM((K, 2, CH, BS), BF),
        pltpu.VMEM((4, 32, 512), F32),
        pltpu.VMEM((4, 32, 512), F32),
        pltpu.VMEM((4, 8, 512), F32),
        pltpu.VMEM((4, 8, 512), F32),
        pltpu.VMEM((4, 8, 512), F32),
        pltpu.VMEM((4, 8, 512), F32),
        pltpu.SemaphoreType.DMA,
    ]
    scratch += [dma(*per_chunk) for _ in range(11)]
    scratch += [dma(K, 4, 4), dma(K, 4, 4), dma(K, 4, 3), dma(K, 4, 3), dma(1), dma(1), dma(4, 2), dma(4, 2)]
    scratch += [dma(K, 4, 4), dma(K, 4, 4)]
    scratch += [dma(*per_chunk) for _ in range(16)] + [dma(K, 2) for _ in range(4)]
    scratch += [dma(4) for _ in range(10)]
    act_t, gf_t, grad_weight = pl.pallas_call(
        kernel,
        out_shape=(
            jax.ShapeDtypeStruct((4, FS, BS), BF),
            jax.ShapeDtypeStruct((4, FS, BS), F32),
            jax.ShapeDtypeStruct((FS, 512), F32),
        ),
        in_specs=[pl.BlockSpec(memory_space=pltpu.SMEM)] + [vm] * 5 + [pl.BlockSpec(memory_space=pl.ANY)],
        out_specs=(vm, vm, vm),
        scratch_shapes=scratch,
        compiler_params=pltpu.CompilerParams(
            collective_id=0, has_side_effects=True, vmem_limit_bytes=56 << 20
        ),
        cost_estimate=pl.CostEstimate(flops=4_000_000_000, bytes_accessed=13_000_000, transcendentals=300_000),
    )(tile_counts, block_rows[0], block_cols[0], features, weight, cotangent, blocks)
    return pl.pallas_call(
        write_out,
        out_shape=(
            jax.ShapeDtypeStruct(features.shape, BF),
            jax.ShapeDtypeStruct(features.shape, BF),
            jax.ShapeDtypeStruct((FS, 512), F32),
        ),
        in_specs=[vm] * 3,
        out_specs=(vm, vm, vm),
        cost_estimate=pl.CostEstimate(flops=0, bytes_accessed=2_000_000, transcendentals=0),
    )(act_t, gf_t, grad_weight)


def solution(mesh):
    in_specs = (
        P(("row", "col"), "depth"),
        P(),
        P(("row", "col"), "depth"),
        P("row", "col", None, None, None),
        P("row", "col", None),
        P("row", "col", None),
        P("row", "col"),
    )
    out_specs = (P(("row", "col"), "depth"), P(("row", "col"), "depth"), P("depth", None))
    return jax.shard_map(layer, mesh=mesh, in_specs=in_specs, out_specs=out_specs, check_vma=False)
```

```python
import jax
import jax.numpy as jnp
from jax import lax
from jax.experimental import pallas as pl
from jax.experimental.pallas import tpu as pltpu
from jax.sharding import PartitionSpec as P

BF = jnp.bfloat16
F32 = jnp.float32
K = 2
CH = 64
BS = 256
PB = 1
NP = 4 // PB
FS = 128
GC = 0.7978845608028654
NB = 80
PF, CF, KF, LF, QB, RB, KB, LB = range(8)


def slot_order(major, minor, span, valid):
    side = major.shape[0]
    lane = lax.broadcasted_iota(jnp.int32, (side, side), 1)
    key = jnp.where(valid, major * span + minor, 4096 + lane)
    key_t, major_t, minor_t = key.T, major.T, minor.T
    valid_t = valid.astype(jnp.int32).T > 0
    rank = jnp.sum((key < key_t).astype(jnp.int32), axis=1, keepdims=True)
    at = lax.broadcasted_iota(jnp.int32, (side, side), 0)

    def pick(cond, value):
        return jnp.sum(jnp.where(cond, value, 0), axis=0, keepdims=True)

    hit = rank == lane
    perm = pick(hit, at)
    minor_sorted = pick(hit, minor_t)
    major_sorted = pick(hit, major_t + 1)
    before = pick(rank + 1 == lane, major_t + 1)
    keep = (major_sorted == before).astype(jnp.int32)
    ends = pick(valid_t & (major_t <= lane), 1)
    used = pick(valid_t & (major_t == lane), 1)
    last = jnp.where(used > 0, ends - 1, -1)
    return [perm, minor_sorted, keep, last]


def kernel(
    count, rows_of, cols_of, feat, weight, cot, adj_hbm,
    act_out, gf_out, gw_out,
    idx, table, idx_sem,
    adj, gath, work, buf, part, yrecv, agg, cott, gmix, wt,
    tgt, terms, xfl, xfr, xol, xor_, lines, zfd, zfu, z3d, z3u, xo3, xf3,
    gw, gwy, gwx, gwxr, gwz, gwxa,
    adj_sem,
    zsu, zsd, zr, xsr, xsl, xrl, xrr, osr, osl, orl, orr,
    ys, yr, ds, dr, cs, cr, gs, gr, ts, tr,
    asr, asl, arl, arr, bsr, bsl, brl, brr, us, dns, ur, dnr,
    u3s, d3s, u3r, d3r, o3s, o3r, f3s, f3r,
    wys, wyr, wxs, wxr, wzs, wzr, vxs, vxr, vys, vyr,
):
    row = lax.axis_index("row")
    c = lax.axis_index("col")
    d = lax.axis_index("depth")
    x, z = row // 4, row % 4
    zh, core = d // 2, d % 2
    right = {"row": (x + 1) % 4 * 4 + z}
    left = {"row": (x + 3) % 4 * 4 + z}
    up = {"row": x * 4 + (z + 1) % 4}
    down = {"row": x * 4 + (z + 3) % 4}
    d_core = zh * 2 + (1 - core)
    d_far = (1 - zh) * 2 + core
    d_diag = (1 - zh) * 2 + (1 - core)
    to_core = {"depth": d_core}
    to_far = {"depth": d_far}
    xr1, xl1, xop = (x + 1) % 4, (x + 3) % 4, (x + 2) % 4

    def rcopy(src, dst, ssem, rsem, dev):
        return pltpu.make_async_remote_copy(
            src_ref=src, dst_ref=dst, send_sem=ssem, recv_sem=rsem,
            device_id=dev, device_id_type=pl.DeviceIdType.MESH,
        )

    def go(op, *args):
        copy = rcopy(*args)
        if op == "start":
            copy.start()
        elif op == "sent":
            copy.wait_send()
        else:
            copy.wait_recv()

    barrier = pltpu.get_barrier_semaphore()
    for o in range(1, 4):
        for dev in (
            {"row": (x + o) % 4 * 4 + z},
            {"row": x * 4 + (z + o) % 4},
            {"col": (c + o) % 4},
        ):
            pl.semaphore_signal(barrier, inc=1, device_id=dev, device_id_type=pl.DeviceIdType.MESH)
    for dev in (to_core, to_far):
        pl.semaphore_signal(barrier, inc=1, device_id=dev, device_id_type=pl.DeviceIdType.MESH)

    adj_copy = pltpu.make_async_copy(adj_hbm, adj, adj_sem)
    adj_copy.start()

    for b in range(4):
        flip = feat[b * BS:(b + 1) * BS, :].astype(F32).T.astype(BF)
        for k in range(K):
            gath[k, row * 4 + b] = flip[k * CH:(k + 1) * CH]

    pl.semaphore_wait(barrier, 11)

    def shard(k, xx, zz):
        return gath.at[k, pl.ds((xx * 4 + zz) * 4, 4)]

    def lower(k, xx, zz):
        return gath.at[k, pl.ds((xx * 4 + zz) * 4, 2)]

    def upper(k, xx, zz):
        return gath.at[k, pl.ds((xx * 4 + zz) * 4 + 2, 2)]

    def z_up(op, k, zz):
        go(op, shard(k, x, zz), shard(k, x, zz), zsu.at[k, zz], zr.at[k, zz], up)

    def z_down(op, k, zz):
        go(op, shard(k, x, zz), shard(k, x, zz), zsd.at[k, zz], zr.at[k, zz], down)

    def z_own(op, k):
        @pl.when(z < 3)
        def _():
            z_up(op, k, z)

        @pl.when(z > 0)
        def _():
            z_down(op, k, z)

    def x_send(op, k, zz):
        go(op, shard(k, x, zz), shard(k, x, zz), xsr.at[k, zz], xrl.at[k, zz], right)
        go(op, shard(k, x, zz), shard(k, x, zz), xsl.at[k, zz], xrr.at[k, zz], left)

    def z_stage(op, first, count=1):
        for o in range(1, 4):
            @pl.when(z >= o)
            def _():
                zz = z - o

                def one(k, _):
                    if op == "start":
                        z_up("recv", k, zz)

                    @pl.when(z < 3)
                    def _():
                        z_up(op, k, zz)
                    x_send(op, k, zz)
                    return 0
                lax.fori_loop(first, first + count, one, 0)

            @pl.when(z + o <= 3)
            def _():
                zz = z + o

                def one(k, _):
                    if op == "start":
                        z_down("recv", k, zz)

                    @pl.when(z > 0)
                    def _():
                        z_down(op, k, zz)
                    x_send(op, k, zz)
                    return 0
                lax.fori_loop(first, first + count, one, 0)

    def x_pass(op, k):
        def one(i, _):
            zz = (z + i) % 4
            if op == "start":
                go("recv", shard(k, xl1, zz), shard(k, xl1, zz), xsr.at[k, zz], xrl.at[k, zz], right)
            go(op, lower(k, xl1, zz), lower(k, xl1, zz), osr.at[k, zz], orl.at[k, zz], right)
            if op == "start":
                go("recv", shard(k, xr1, zz), shard(k, xr1, zz), xsl.at[k, zz], xrr.at[k, zz], left)
            go(op, upper(k, xr1, zz), upper(k, xr1, zz), osl.at[k, zz], orr.at[k, zz], left)
            return 0
        lax.fori_loop(0, 4, one, 0)

    def x_last(k):
        def one(i, _):
            zz = (z + i) % 4
            go("recv", lower(k, xop, zz), lower(k, xop, zz), osr.at[k, zz], orl.at[k, zz], right)
            go("recv", upper(k, xop, zz), upper(k, xop, zz), osl.at[k, zz], orr.at[k, zz], left)
            return 0
        lax.fori_loop(0, 4, one, 0)

    def y_send(op, k, p):
        for o in range(1, 4):
            to = (c + o) % 4
            go(
                op, part.at[k, pl.ds(to * 4 + p * PB, PB)], yrecv.at[k, c, pl.ds(p * PB, PB)],
                ys.at[k, p, o], yr.at[k, p, c], {"col": to},
            )

    def y_sum(k, p):
        for o in range(1, 4):
            src = (c + o) % 4
            go(
                "recv", part.at[k, pl.ds(c * 4 + p * PB, PB)], yrecv.at[k, src, pl.ds(p * PB, PB)],
                ys.at[k, p, o], yr.at[k, p, src], {"col": src},
            )
        for q in range(PB):
            b = p * PB + q
            total = part[k, c * 4 + b].astype(F32)
            for o in range(1, 4):
                total = total + yrecv[k, (c + o) % 4, b].astype(F32)
            agg[b, pl.ds(pl.multiple_of(d * FS + k * CH, CH), CH), :] = total.astype(BF)

    def agg_rows(dd, k, p):
        return agg.at[pl.ds(p * PB, PB), pl.ds(pl.multiple_of(dd * FS + k * CH, CH), CH), :]

    def d_send(op, k, p):
        own = agg_rows(d, k, p)
        go(op, own, own, ds.at[k, p, 1], dr.at[k, p, 1], to_far)
        go(op, own, own, ds.at[k, p, 0], dr.at[k, p, 0], to_core)

    def d_pass(op, k, p):
        far = agg_rows(d_far, k, p)
        if op == "start":
            go("recv", far, far, ds.at[k, p, 1], dr.at[k, p, 1], to_far)
        go(op, far, far, ds.at[k, p, 2], dr.at[k, p, 2], to_core)

    def d_last(k, p):
        near, diag = agg_rows(d_core, k, p), agg_rows(d_diag, k, p)
        go("recv", near, near, ds.at[k, p, 0], dr.at[k, p, 0], to_core)
        go("recv", diag, diag, ds.at[k, p, 2], dr.at[k, p, 2], to_core)

    def blocks(fn, *args):
        def one(p, _):
            fn(*args, p)
            return 0
        lax.fori_loop(0, NP, one, 0)

    def cot_send(op):
        go(op, cott.at[zh], cott.at[zh], cs.at[0], cr.at[0], to_far)

    def forward_tile(k):
        def move(i, _):
            work[i] = gath[k, i]
            return 0
        lax.fori_loop(0, 64, move, 0, unroll=4)

        def slot(s, acc):
            prod = lax.dot_general(
                work[idx[CF, s]], adj[idx[PF, s]], (((1,), (1,)), ((), ())),
                preferred_element_type=F32,
            )
            acc = acc * idx[KF, s].astype(F32) + prod
            buf[s] = acc.astype(BF)
            return acc
        lax.fori_loop(0, NB, slot, jnp.zeros((CH, BS), F32), unroll=16)

        def pick(p, _):
            for q in range(4):
                for e in range(PB):
                    i = q * 4 + p * PB + e
                    last = idx[LF, i]
                    on = (jnp.minimum(last, 0) + 1).astype(F32)
                    part[k, i] = (buf[jnp.maximum(last, 0)].astype(F32) * on).astype(BF)
            y_send("start", k, p)
            return 0
        lax.fori_loop(0, NP, pick, 0)

    for k in range(min(2, K)):
        z_own("start", k)
        x_send("start", k, z)

    table[0:2, :] = jnp.zeros((2, 128), jnp.int32)
    table[0:1, 0:NB] = rows_of[...]
    table[1:2, 0:NB] = cols_of[...]
    rows_all = jnp.broadcast_to(table[0:1, :], (128, 128))
    cols_all = jnp.broadcast_to(table[1:2, :], (128, 128))
    valid = lax.broadcasted_iota(jnp.int32, (128, 128), 1) < count[0, 0]
    order = slot_order(rows_all, cols_all, 64, valid) + slot_order(cols_all, rows_all, 16, valid)
    for i in range(8):
        table[i:i + 1, :] = order[i]
    idx_copy = pltpu.make_async_copy(table, idx, idx_sem)
    idx_copy.start()

    for b in range(4):
        cott[zh, b] = cot[b * BS:(b + 1) * BS, :].astype(F32).T.astype(BF)
    z_stage("start", 0, K)
    if K == 2:
        cot_send("start")
    for i in range(2):
        for j in range(4):
            cols = pl.ds(pl.multiple_of((i * 2 + core) * FS, FS), FS)
            wt[i, :, j * FS:(j + 1) * FS] = weight[j * FS:(j + 1) * FS, cols].astype(F32).T.astype(BF)
    x_pass("start", 0)
    idx_copy.wait()
    adj_copy.wait()

    def forward_step(k, _):
        @pl.when(k + 2 < K)
        def _():
            z_own("start", k + 2)
            x_send("start", k + 2, z)
            z_stage("start", k + 2)

        @pl.when(k + 3 == K)
        def _():
            cot_send("start")

        @pl.when(k + 1 < K)
        def _():
            x_pass("start", k + 1)

        @pl.when(k > 0)
        def _():
            def one(p, _):
                y_sum(k - 1, p)
                d_send("start", k - 1, p)
                return 0
            lax.fori_loop(0, NP, one, 0)
        x_last(k)

        forward_tile(k)

        @pl.when(k > 0)
        def _():
            blocks(d_pass, "start", k - 1)
        return 0
    lax.fori_loop(0, K, forward_step, 0)

    def last_sum(p, _):
        y_sum(K - 1, p)
        d_send("start", K - 1, p)
        return 0
    lax.fori_loop(0, NP, last_sum, 0)
    go("recv", cott.at[1 - zh], cott.at[1 - zh], cs.at[0], cr.at[0], to_far)

    def mix_rows(p, dd):
        return gmix.at[pl.ds(p * PB, PB), pl.ds(pl.multiple_of(dd * FS, FS), FS), :]

    def mix_send(op, p):
        go(op, mix_rows(p, d), mix_rows(p, d), gs.at[p, 0], gr.at[p, 0], to_core)
        go(op, mix_rows(p, d_far), mix_rows(p, d_far), gs.at[p, 1], gr.at[p, 1], to_core)

    def mix_last(p):
        go("recv", mix_rows(p, d_core), mix_rows(p, d_core), gs.at[p, 0], gr.at[p, 0], to_core)
        go("recv", mix_rows(p, d_diag), mix_rows(p, d_diag), gs.at[p, 1], gr.at[p, 1], to_core)

    def dense(b):
        for own in (True, False):
            at = zh if own else 1 - zh
            dd = at * 2 + core
            m = jnp.dot(wt[at], agg[b], preferred_element_type=F32)
            sq = m * m
            t = jnp.tanh(GC * (m + 0.044715 * (sq * m)))
            half = 0.5 + 0.5 * t
            if own:
                act_out[b] = (m * half).astype(BF)
            slope = half + 0.5 * m * (1.0 - t * t) * (GC + (3 * 0.044715 * GC) * sq)
            gmix[b, pl.ds(pl.multiple_of(dd * FS, FS), FS), :] = (
                cott[at, b].astype(F32) * slope
            ).astype(BF)

    def back_mix(p):
        mix_last(p)

        def one(q, _):
            b = p * PB + q
            ga = jnp.dot(
                weight[pl.ds(pl.multiple_of(d * FS, FS), FS), :], gmix[b], preferred_element_type=F32
            ).astype(BF)
            for k in range(K):
                tgt[k, c * 4 + b] = ga[k * CH:(k + 1) * CH]
            return 0
        lax.fori_loop(0, PB, one, 0)
        t_send("start", 0, p)

    def t_send(op, k, p):
        own = tgt.at[k, pl.ds(c * 4 + p * PB, PB)]
        for o in range(1, 4):
            go(op, own, own, ts.at[k, p, o], tr.at[k, p, c], {"col": (c + o) % 4})

    def t_last(k):
        def one(p, _):
            for o in range(1, 4):
                src = (c + o) % 4
                ref = tgt.at[k, pl.ds(src * 4 + p * PB, PB)]
                go("recv", ref, ref, ts.at[k, p, o], tr.at[k, p, src], {"col": src})
            return 0
        lax.fori_loop(0, NP, one, 0)

    d_pass("start", K - 1, 0)

    def middle(p, _):
        @pl.when(p < NP - 1)
        def _():
            d_pass("start", K - 1, p + 1)
        for k in range(K):
            d_last(k, p)

        def one(q, _):
            dense(p * PB + q)
            return 0
        lax.fori_loop(0, PB, one, 0)
        mix_send("start", p)

        @pl.when(p > 0)
        def _():
            back_mix(p - 1)
        return 0
    lax.fori_loop(0, NP, middle, 0)
    back_mix(NP - 1)
    for k in range(1, K):
        blocks(t_send, "start", k)

    def gw_block(b, _):
        own = agg[b, pl.ds(pl.multiple_of(d * FS, FS), FS), :]
        for j in range(2):
            add = lax.dot_general(
                own, gmix[b, j * 256:(j + 1) * 256, :], (((1,), (1,)), ((), ())),
                preferred_element_type=F32,
            )
            for q in range(4):
                gw[q, :, j * 256:(j + 1) * 256] += add[q * 32:(q + 1) * 32]
        return 0
    gw[...] = jnp.zeros_like(gw)
    lax.fori_loop(0, 4, gw_block, 0)

    def wy(op, o):
        to = (c + o) % 4
        go(op, gw.at[to], gwy.at[c], wys.at[o], wyr.at[c], {"col": to})

    def wx(op, o):
        to = (x + o) % 4
        go(op, gwx.at[to], gwxr.at[x], wxs.at[o], wxr.at[x], {"row": to * 4 + z})

    def wz(op, o):
        go(op, gwz.at[z], gwz.at[z], wzs.at[o], wzr.at[z], {"row": x * 4 + (z + o) % 4})

    def vx(op, o):
        go(op, gwxa.at[x], gwxa.at[x], vxs.at[o], vxr.at[x], {"row": (x + o) % 4 * 4 + z})

    def vy(op, o):
        own = gw_out.at[pl.ds(pl.multiple_of(c * 32, 32), 32), :]
        go(op, own, own, vys.at[o], vyr.at[c], {"col": (c + o) % 4})

    def all3(fn, op):
        for o in range(1, 4):
            fn(op, o)

    def weight_step(it):
        if it == 1:
            for o in range(1, 4):
                src = (c + o) % 4
                go("recv", gw.at[c], gwy.at[src], wys.at[o], wyr.at[src], {"col": src})
            total = gw[c]
            for o in range(1, 4):
                total = total + gwy[(c + o) % 4]
            for q in range(4):
                gwx[q] = total[q * 8:(q + 1) * 8]
            all3(wx, "start")

        if it == 2:
            for o in range(1, 4):
                src = (x + o) % 4
                go("recv", gwx.at[x], gwxr.at[src], wxs.at[o], wxr.at[src], right)
            total = gwx[x]
            for o in range(1, 4):
                total = total + gwxr[(x + o) % 4]
            gwz[z] = total
            all3(wz, "start")

        if it == 3:
            for o in range(1, 4):
                src = (z + o) % 4
                go("recv", gwz.at[src], gwz.at[src], wzs.at[o], wzr.at[src], up)
            gwxa[x] = (gwz[0] + gwz[1]) + (gwz[2] + gwz[3])
            all3(vx, "start")

        if it == 4:
            for o in range(1, 4):
                src = (x + o) % 4
                go("recv", gwxa.at[src], gwxa.at[src], vxs.at[o], vxr.at[src], right)
            for q in range(4):
                gw_out[pl.ds(pl.multiple_of(c * 32 + q * 8, 8), 8), :] = gwxa[q]
            all3(vy, "start")

    all3(wy, "start")

    def backward_tile(k):
        t_last(k)

        def move(i, _):
            work[i] = tgt[k, i]
            return 0
        lax.fori_loop(0, 16, move, 0, unroll=4)

        def slot(s, acc):
            prod = jnp.dot(work[idx[RB, s]], adj[idx[QB, s]], preferred_element_type=F32)
            acc = acc * idx[KB, s].astype(F32) + prod
            buf[s] = acc.astype(BF)
            return acc
        lax.fori_loop(0, NB, slot, jnp.zeros((CH, BS), F32), unroll=16)

        def pick(i, _):
            last = idx[LB, i]
            on = (jnp.minimum(last, 0) + 1).astype(F32)
            terms[k, i // 16, i // 4 % 4, i % 4] = (buf[jnp.maximum(last, 0)].astype(F32) * on).astype(BF)
            return 0
        lax.fori_loop(0, 64, pick, 0, unroll=4)

    HALF = CH // 2
    order = (3, 0, 2, 1)

    def add_to(ref, at, got):
        ref[at] = (ref[at].astype(F32) + got.astype(F32)).astype(BF)

    def term(k, xx, zz, lo=0, n=CH):
        return terms.at[k, xx, zz, pl.ds(0, 3), pl.ds(lo, n)]

    def far_half(op, k):
        for zz in order:
            go(op, term(k, xop, zz, 0, HALF), xol.at[k, zz], asr.at[k, zz], arl.at[k, zz], right)
            go(op, term(k, xop, zz, HALF, HALF), xor_.at[k, zz], asl.at[k, zz], arr.at[k, zz], left)

    def near_full(op, k):
        for zz in order:
            if op == "start":
                go("recv", term(k, xop, zz, 0, HALF), xol.at[k, zz], asr.at[k, zz], arl.at[k, zz], right)
                for b in range(3):
                    add_to(terms, (k, xr1, zz, b, slice(0, HALF)), xol[k, zz, b])
            go(op, term(k, xr1, zz), xfl.at[k, zz], bsr.at[k, zz], brl.at[k, zz], right)
            if op == "start":
                go("recv", term(k, xop, zz, HALF, HALF), xor_.at[k, zz], asl.at[k, zz], arr.at[k, zz], left)
                for b in range(3):
                    add_to(terms, (k, xl1, zz, b, slice(HALF, CH)), xor_[k, zz, b])
            go(op, term(k, xl1, zz), xfr.at[k, zz], bsl.at[k, zz], brr.at[k, zz], left)

    def x_sum(k):
        for zz in order:
            go("recv", term(k, xr1, zz), xfl.at[k, zz], bsr.at[k, zz], brl.at[k, zz], right)
            go("recv", term(k, xl1, zz), xfr.at[k, zz], bsl.at[k, zz], brr.at[k, zz], left)
            for b in range(3):
                lines[k, zz, b] = (
                    terms[k, x, zz, b].astype(F32) + xfl[k, zz, b].astype(F32) + xfr[k, zz, b].astype(F32)
                ).astype(BF)
            if zz > 0:
                @pl.when(z == 0)
                def _():
                    up_msg("start", k, zz)
            if zz < 3:
                @pl.when(z == 3)
                def _():
                    down_msg("start", k, zz)

    def up_msg(op, k, zz):
        go(op, lines.at[k, zz], zfd.at[k, zz], us.at[k, zz], dnr.at[k, zz], up)

    def down_msg(op, k, zz):
        go(op, lines.at[k, zz], zfu.at[k, zz], dns.at[k, zz], ur.at[k, zz], down)

    def pass_on(op, k):
        for at, zz in ((1, 3), (1, 2), (2, 3)):
            @pl.when(z == at)
            def _():
                if op == "start":
                    up_msg("recv", k, zz)
                    for b in range(3):
                        add_to(lines, (k, zz, b), zfd[k, zz, b])
                up_msg(op, k, zz)

            @pl.when(z == 3 - at)
            def _():
                if op == "start":
                    down_msg("recv", k, 3 - zz)
                    for b in range(3):
                        add_to(lines, (k, 3 - zz, b), zfu[k, 3 - zz, b])
                down_msg(op, k, 3 - zz)

    def x_sum_sent(k):
        for zz in (1, 2, 3):
            @pl.when(z == 0)
            def _():
                up_msg("sent", k, zz)

            @pl.when(z == 3)
            def _():
                down_msg("sent", k, 3 - zz)

    def finish(k):
        rows = pl.ds(k * CH, CH)
        for b in range(3):
            gf_out[b, rows, :] = lines[k, z, b].astype(F32)

        @pl.when(z > 0)
        def _():
            up_msg("recv", k, z)
            for b in range(3):
                gf_out[b, rows, :] += zfd[k, z, b].astype(F32)

        @pl.when(z < 3)
        def _():
            down_msg("recv", k, z)
            for b in range(3):
                gf_out[b, rows, :] += zfu[k, z, b].astype(F32)

    def up3(op, k, zz):
        go(op, terms.at[k, :, zz, 3], z3d.at[k, zz], u3s.at[k, zz], d3r.at[k, zz], up)

    def down3(op, k, zz):
        go(op, terms.at[k, :, zz, 3], z3u.at[k, zz], d3s.at[k, zz], u3r.at[k, zz], down)

    def line3(op, k, stage):
        for zz in range(3, stage, -1):
            @pl.when(z == stage)
            def _():
                if op == "start" and stage > 0:
                    up3("recv", k, zz)
                    for q in range(4):
                        add_to(terms, (k, q, zz, 3), z3d[k, zz, q])
                up3(op, k, zz)

            @pl.when(z == 3 - stage)
            def _():
                if op == "start" and stage > 0:
                    down3("recv", k, 3 - zz)
                    for q in range(4):
                        add_to(terms, (k, q, 3 - zz, 3), z3u[k, 3 - zz, q])
                down3(op, k, 3 - zz)

    def line3_sum(k):
        @pl.when(z > 0)
        def _():
            up3("recv", k, z)
            for q in range(4):
                add_to(terms, (k, q, z, 3), z3d[k, z, q])

        @pl.when(z < 3)
        def _():
            down3("recv", k, z)
            for q in range(4):
                add_to(terms, (k, q, z, 3), z3u[k, z, q])

    def one3(k, xx, lo=0, n=CH):
        return terms.at[k, xx, z, 3, pl.ds(lo, n)]

    def far3(op, k):
        go(op, one3(k, xop, 0, HALF), xo3.at[k, 0], o3s.at[k, 0], o3r.at[k, 0], right)
        go(op, one3(k, xop, HALF, HALF), xo3.at[k, 1], o3s.at[k, 1], o3r.at[k, 1], left)

    def near3(op, k):
        if op == "start":
            go("recv", one3(k, xop, 0, HALF), xo3.at[k, 0], o3s.at[k, 0], o3r.at[k, 0], right)
            add_to(terms, (k, xr1, z, 3, slice(0, HALF)), xo3[k, 0])
        go(op, one3(k, xr1), xf3.at[k, 0], f3s.at[k, 0], f3r.at[k, 0], right)
        if op == "start":
            go("recv", one3(k, xop, HALF, HALF), xo3.at[k, 1], o3s.at[k, 1], o3r.at[k, 1], left)
            add_to(terms, (k, xl1, z, 3, slice(HALF, CH)), xo3[k, 1])
        go(op, one3(k, xl1), xf3.at[k, 1], f3s.at[k, 1], f3r.at[k, 1], left)

    def finish3(k):
        go("recv", one3(k, xr1), xf3.at[k, 0], f3s.at[k, 0], f3r.at[k, 0], right)
        go("recv", one3(k, xl1), xf3.at[k, 1], f3s.at[k, 1], f3r.at[k, 1], left)
        gf_out[3, k * CH:(k + 1) * CH, :] = (
            terms[k, x, z, 3].astype(F32) + xf3[k, 0].astype(F32) + xf3[k, 1].astype(F32)
        )

    backward_tile(0)
    far_half("start", 0)
    line3("start", 0, 0)
    backward_tile(1)
    line3("start", 1, 0)
    line3("start", 0, 1)
    near_full("start", 0)
    far_half("start", 1)
    line3("start", 0, 2)
    weight_step(1)
    line3("start", 1, 1)
    line3_sum(0)
    far3("start", 0)
    line3("start", 1, 2)
    x_sum(0)
    near_full("start", 1)
    near3("start", 0)
    line3_sum(1)
    far3("start", 1)
    weight_step(2)
    pass_on("start", 0)
    near3("start", 1)
    finish3(0)
    weight_step(3)
    finish(0)
    finish3(1)
    weight_step(4)
    def drain(k, _):
        z_own("sent", k)
        x_send("sent", k, z)
        z_stage("sent", k)
        x_pass("sent", k)
        for fn in (y_send, d_send, d_pass, t_send):
            blocks(fn, "sent", k)
        far_half("sent", k)
        for stage in range(3):
            line3("sent", k, stage)
        far3("sent", k)
        near3("sent", k)
        return 0
    lax.fori_loop(0, K, drain, 0)
    near_full("sent", 0)
    x_sum_sent(0)
    pass_on("sent", 0)
    blocks(mix_send, "sent")
    cot_send("sent")
    for fn in (wy, wx, wz, vx):
        all3(fn, "sent")

    x_sum(1)
    pass_on("start", 1)
    finish(1)

    for o in range(1, 4):
        src = (c + o) % 4
        ref = gw_out.at[pl.ds(pl.multiple_of(src * 32, 32), 32), :]
        go("recv", ref, ref, vys.at[o], vyr.at[src], {"col": src})

    near_full("sent", K - 1)
    x_sum_sent(K - 1)
    pass_on("sent", K - 1)
    all3(vy, "sent")


def write_out(act_t, gf_t, gw, act, gf, gw_out):
    gw_out[...] = gw[...]
    for b in range(4):
        act[b * BS:(b + 1) * BS, :] = act_t[b].astype(F32).T.astype(BF)
        gf[b * BS:(b + 1) * BS, :] = gf_t[b].T.astype(BF)


def layer(features, weight, cotangent, adjacency_blocks, block_rows, block_cols, tile_counts):
    blocks = adjacency_blocks[0, 0]
    vm = pl.BlockSpec(memory_space=pltpu.VMEM)
    dma = lambda *s: pltpu.SemaphoreType.DMA(s)
    per_chunk = (K, 4)
    scratch = [
        pltpu.SMEM((8, 128), jnp.int32),
        pltpu.VMEM((8, 128), jnp.int32),
        pltpu.SemaphoreType.DMA,
        pltpu.VMEM((NB, BS, BS), BF),
        pltpu.VMEM((K, 64, CH, BS), BF),
        pltpu.VMEM((64, CH, BS), BF),
        pltpu.VMEM((NB, CH, BS), BF),
        pltpu.VMEM((K, 16, CH, BS), BF),
        pltpu.VMEM((K, 4, 4, CH, BS), BF),
        pltpu.VMEM((4, 512, BS), BF),
        pltpu.VMEM((2, 4, FS, BS), BF),
        pltpu.VMEM((4, 512, BS), BF),
        pltpu.VMEM((2, FS, 512), BF),
        pltpu.VMEM((K, 16, CH, BS), BF),
        pltpu.VMEM((K, 4, 4, 4, CH, BS), BF),
        pltpu.VMEM((K, 4, 3, CH, BS), BF),
        pltpu.VMEM((K, 4, 3, CH, BS), BF),
        pltpu.VMEM((K, 4, 3, CH // 2, BS), BF),
        pltpu.VMEM((K, 4, 3, CH // 2, BS), BF),
        pltpu.VMEM((K, 4, 3, CH, BS), BF),
        pltpu.VMEM((K, 4, 3, CH, BS), BF),
        pltpu.VMEM((K, 4, 3, CH, BS), BF),
        pltpu.VMEM((K, 4, 4, CH, BS), BF),
        pltpu.VMEM((K, 4, 4, CH, BS), BF),
        pltpu.VMEM((K, 2, CH // 2, BS), BF),
        pltpu.VMEM((K, 2, CH, BS), BF),
        pltpu.VMEM((4, 32, 512), F32),
        pltpu.VMEM((4, 32, 512), F32),
        pltpu.VMEM((4, 8, 512), F32),
        pltpu.VMEM((4, 8, 512), F32),
        pltpu.VMEM((4, 8, 512), F32),
        pltpu.VMEM((4, 8, 512), F32),
        pltpu.SemaphoreType.DMA,
    ]
    scratch += [dma(*per_chunk) for _ in range(11)]
    scratch += [dma(K, 4, 4), dma(K, 4, 4), dma(K, 4, 3), dma(K, 4, 3), dma(1), dma(1), dma(4, 2), dma(4, 2)]
    scratch += [dma(K, 4, 4), dma(K, 4, 4)]
    scratch += [dma(*per_chunk) for _ in range(16)] + [dma(K, 2) for _ in range(4)]
    scratch += [dma(4) for _ in range(10)]
    act_t, gf_t, grad_weight = pl.pallas_call(
        kernel,
        out_shape=(
            jax.ShapeDtypeStruct((4, FS, BS), BF),
            jax.ShapeDtypeStruct((4, FS, BS), F32),
            jax.ShapeDtypeStruct((FS, 512), F32),
        ),
        in_specs=[pl.BlockSpec(memory_space=pltpu.SMEM)] + [vm] * 5 + [pl.BlockSpec(memory_space=pl.ANY)],
        out_specs=(vm, vm, vm),
        scratch_shapes=scratch,
        compiler_params=pltpu.CompilerParams(
            collective_id=0, has_side_effects=True, vmem_limit_bytes=56 << 20
        ),
        cost_estimate=pl.CostEstimate(flops=4_000_000_000, bytes_accessed=13_000_000, transcendentals=300_000),
    )(tile_counts, block_rows[0], block_cols[0], features, weight, cotangent, blocks)
    return pl.pallas_call(
        write_out,
        out_shape=(
            jax.ShapeDtypeStruct(features.shape, BF),
            jax.ShapeDtypeStruct(features.shape, BF),
            jax.ShapeDtypeStruct((FS, 512), F32),
        ),
        in_specs=[vm] * 3,
        out_specs=(vm, vm, vm),
        cost_estimate=pl.CostEstimate(flops=0, bytes_accessed=2_000_000, transcendentals=0),
    )(act_t, gf_t, grad_weight)


def solution(mesh):
    in_specs = (
        P(("row", "col"), "depth"),
        P(),
        P(("row", "col"), "depth"),
        P("row", "col", None, None, None),
        P("row", "col", None),
        P("row", "col", None),
        P("row", "col"),
    )
    out_specs = (P(("row", "col"), "depth"), P(("row", "col"), "depth"), P("depth", None))
    return jax.shard_map(layer, mesh=mesh, in_specs=in_specs, out_specs=out_specs, check_vma=False)
```

```python
import jax
import jax.numpy as jnp
from jax import lax
from jax.experimental import pallas as pl
from jax.experimental.pallas import tpu as pltpu
from jax.sharding import PartitionSpec as P

BF = jnp.bfloat16
F32 = jnp.float32
K = 2
CH = 64
BS = 256
PB = 1
NP = 4 // PB
FS = 128
GC = 0.7978845608028654
NB = 80
PF, CF, KF, LF, QB, RB, KB, LB = range(8)


def slot_order(major, minor, span, valid):
    side = major.shape[0]
    lane = lax.broadcasted_iota(jnp.int32, (side, side), 1)
    key = jnp.where(valid, major * span + minor, 4096 + lane)
    key_t, major_t, minor_t = key.T, major.T, minor.T
    valid_t = valid.astype(jnp.int32).T > 0
    rank = jnp.sum((key < key_t).astype(jnp.int32), axis=1, keepdims=True)
    at = lax.broadcasted_iota(jnp.int32, (side, side), 0)

    def pick(cond, value):
        return jnp.sum(jnp.where(cond, value, 0), axis=0, keepdims=True)

    hit = rank == lane
    perm = pick(hit, at)
    minor_sorted = pick(hit, minor_t)
    major_sorted = pick(hit, major_t + 1)
    before = pick(rank + 1 == lane, major_t + 1)
    keep = (major_sorted == before).astype(jnp.int32)
    ends = pick(valid_t & (major_t <= lane), 1)
    used = pick(valid_t & (major_t == lane), 1)
    last = jnp.where(used > 0, ends - 1, -1)
    return [perm, minor_sorted, keep, last]


def kernel(
    count, rows_of, cols_of, feat, weight, cot, adj_hbm,
    act_out, gf_out, gw_out,
    idx, table, idx_sem,
    adj, gath, work, buf, part, yrecv, agg, cott, gmix, wt,
    tgt, terms, xfl, xfr, xol, xor_, lines, zfd, zfu, z3d, z3u, xo3, xf3,
    gw, gwy, gwx, gwxr, gwz, gwxa,
    adj_sem,
    zsu, zsd, zr, xsr, xsl, xrl, xrr, osr, osl, orl, orr,
    ys, yr, ds, dr, cs, cr, gs, gr, ts, tr,
    asr, asl, arl, arr, bsr, bsl, brl, brr, us, dns, ur, dnr,
    u3s, d3s, u3r, d3r, o3s, o3r, f3s, f3r,
    wys, wyr, wxs, wxr, wzs, wzr, vxs, vxr, vys, vyr,
):
    row = lax.axis_index("row")
    c = lax.axis_index("col")
    d = lax.axis_index("depth")
    x, z = row // 4, row % 4
    zh, core = d // 2, d % 2
    right = {"row": (x + 1) % 4 * 4 + z}
    left = {"row": (x + 3) % 4 * 4 + z}
    up = {"row": x * 4 + (z + 1) % 4}
    down = {"row": x * 4 + (z + 3) % 4}
    d_core = zh * 2 + (1 - core)
    d_far = (1 - zh) * 2 + core
    d_diag = (1 - zh) * 2 + (1 - core)
    to_core = {"depth": d_core}
    to_far = {"depth": d_far}
    xr1, xl1, xop = (x + 1) % 4, (x + 3) % 4, (x + 2) % 4

    def rcopy(src, dst, ssem, rsem, dev):
        return pltpu.make_async_remote_copy(
            src_ref=src, dst_ref=dst, send_sem=ssem, recv_sem=rsem,
            device_id=dev, device_id_type=pl.DeviceIdType.MESH,
        )

    def go(op, *args):
        copy = rcopy(*args)
        if op == "start":
            copy.start()
        elif op == "sent":
            copy.wait_send()
        else:
            copy.wait_recv()

    barrier = pltpu.get_barrier_semaphore()
    for o in range(1, 4):
        for dev in (
            {"row": (x + o) % 4 * 4 + z},
            {"row": x * 4 + (z + o) % 4},
            {"col": (c + o) % 4},
        ):
            pl.semaphore_signal(barrier, inc=1, device_id=dev, device_id_type=pl.DeviceIdType.MESH)
    for dev in (to_core, to_far):
        pl.semaphore_signal(barrier, inc=1, device_id=dev, device_id_type=pl.DeviceIdType.MESH)

    adj_copy = pltpu.make_async_copy(adj_hbm, adj, adj_sem)
    adj_copy.start()

    for b in range(4):
        flip = feat[b * BS:(b + 1) * BS, :].astype(F32).T.astype(BF)
        for k in range(K):
            gath[k, row * 4 + b] = flip[k * CH:(k + 1) * CH]

    pl.semaphore_wait(barrier, 11)

    def shard(k, xx, zz):
        return gath.at[k, pl.ds((xx * 4 + zz) * 4, 4)]

    def lower(k, xx, zz):
        return gath.at[k, pl.ds((xx * 4 + zz) * 4, 2)]

    def upper(k, xx, zz):
        return gath.at[k, pl.ds((xx * 4 + zz) * 4 + 2, 2)]

    def z_up(op, k, zz):
        go(op, shard(k, x, zz), shard(k, x, zz), zsu.at[k, zz], zr.at[k, zz], up)

    def z_down(op, k, zz):
        go(op, shard(k, x, zz), shard(k, x, zz), zsd.at[k, zz], zr.at[k, zz], down)

    def z_own(op, k):
        @pl.when(z < 3)
        def _():
            z_up(op, k, z)

        @pl.when(z > 0)
        def _():
            z_down(op, k, z)

    def x_send(op, k, zz):
        go(op, shard(k, x, zz), shard(k, x, zz), xsr.at[k, zz], xrl.at[k, zz], right)
        go(op, shard(k, x, zz), shard(k, x, zz), xsl.at[k, zz], xrr.at[k, zz], left)

    def z_stage(op, first, count=1):
        for o in range(1, 4):
            @pl.when(z >= o)
            def _():
                zz = z - o

                def one(k, _):
                    if op == "start":
                        z_up("recv", k, zz)

                    @pl.when(z < 3)
                    def _():
                        z_up(op, k, zz)
                    x_send(op, k, zz)
                    return 0
                lax.fori_loop(first, first + count, one, 0)

            @pl.when(z + o <= 3)
            def _():
                zz = z + o

                def one(k, _):
                    if op == "start":
                        z_down("recv", k, zz)

                    @pl.when(z > 0)
                    def _():
                        z_down(op, k, zz)
                    x_send(op, k, zz)
                    return 0
                lax.fori_loop(first, first + count, one, 0)

    def x_pass(op, k):
        def one(i, _):
            zz = (z + i) % 4
            if op == "start":
                go("recv", shard(k, xl1, zz), shard(k, xl1, zz), xsr.at[k, zz], xrl.at[k, zz], right)
            go(op, lower(k, xl1, zz), lower(k, xl1, zz), osr.at[k, zz], orl.at[k, zz], right)
            if op == "start":
                go("recv", shard(k, xr1, zz), shard(k, xr1, zz), xsl.at[k, zz], xrr.at[k, zz], left)
            go(op, upper(k, xr1, zz), upper(k, xr1, zz), osl.at[k, zz], orr.at[k, zz], left)
            return 0
        lax.fori_loop(0, 4, one, 0)

    def x_last(k):
        def one(i, _):
            zz = (z + i) % 4
            go("recv", lower(k, xop, zz), lower(k, xop, zz), osr.at[k, zz], orl.at[k, zz], right)
            go("recv", upper(k, xop, zz), upper(k, xop, zz), osl.at[k, zz], orr.at[k, zz], left)
            return 0
        lax.fori_loop(0, 4, one, 0)

    def y_send(op, k, p):
        for o in range(1, 4):
            to = (c + o) % 4
            go(
                op, part.at[k, pl.ds(to * 4 + p * PB, PB)], yrecv.at[k, c, pl.ds(p * PB, PB)],
                ys.at[k, p, o], yr.at[k, p, c], {"col": to},
            )

    def y_sum(k, p):
        for o in range(1, 4):
            src = (c + o) % 4
            go(
                "recv", part.at[k, pl.ds(c * 4 + p * PB, PB)], yrecv.at[k, src, pl.ds(p * PB, PB)],
                ys.at[k, p, o], yr.at[k, p, src], {"col": src},
            )
        for q in range(PB):
            b = p * PB + q
            total = part[k, c * 4 + b].astype(F32)
            for o in range(1, 4):
                total = total + yrecv[k, (c + o) % 4, b].astype(F32)
            agg[b, pl.ds(pl.multiple_of(d * FS + k * CH, CH), CH), :] = total.astype(BF)

    def agg_rows(dd, k, p):
        return agg.at[pl.ds(p * PB, PB), pl.ds(pl.multiple_of(dd * FS + k * CH, CH), CH), :]

    def d_send(op, k, p):
        own = agg_rows(d, k, p)
        go(op, own, own, ds.at[k, p, 1], dr.at[k, p, 1], to_far)
        go(op, own, own, ds.at[k, p, 0], dr.at[k, p, 0], to_core)

    def d_pass(op, k, p):
        far = agg_rows(d_far, k, p)
        if op == "start":
            go("recv", far, far, ds.at[k, p, 1], dr.at[k, p, 1], to_far)
        go(op, far, far, ds.at[k, p, 2], dr.at[k, p, 2], to_core)

    def d_last(k, p):
        near, diag = agg_rows(d_core, k, p), agg_rows(d_diag, k, p)
        go("recv", near, near, ds.at[k, p, 0], dr.at[k, p, 0], to_core)
        go("recv", diag, diag, ds.at[k, p, 2], dr.at[k, p, 2], to_core)

    def blocks(fn, *args):
        def one(p, _):
            fn(*args, p)
            return 0
        lax.fori_loop(0, NP, one, 0)

    def cot_send(op):
        go(op, cott.at[zh], cott.at[zh], cs.at[0], cr.at[0], to_far)

    def forward_tile(k):
        def move(i, _):
            work[i] = gath[k, i]
            return 0
        lax.fori_loop(0, 64, move, 0, unroll=4)

        def slot(s, acc):
            prod = lax.dot_general(
                work[idx[CF, s]], adj[idx[PF, s]], (((1,), (1,)), ((), ())),
                preferred_element_type=F32,
            )
            acc = acc * idx[KF, s].astype(F32) + prod
            buf[s] = acc.astype(BF)
            return acc
        lax.fori_loop(0, NB, slot, jnp.zeros((CH, BS), F32), unroll=16)

        def pick(p, _):
            for q in range(4):
                for e in range(PB):
                    i = q * 4 + p * PB + e
                    last = idx[LF, i]
                    on = (jnp.minimum(last, 0) + 1).astype(F32)
                    part[k, i] = (buf[jnp.maximum(last, 0)].astype(F32) * on).astype(BF)
            y_send("start", k, p)
            return 0
        lax.fori_loop(0, NP, pick, 0)

    for k in range(min(2, K)):
        z_own("start", k)
        x_send("start", k, z)

    table[0:2, :] = jnp.zeros((2, 128), jnp.int32)
    table[0:1, 0:NB] = rows_of[...]
    table[1:2, 0:NB] = cols_of[...]
    rows_all = jnp.broadcast_to(table[0:1, :], (128, 128))
    cols_all = jnp.broadcast_to(table[1:2, :], (128, 128))
    valid = lax.broadcasted_iota(jnp.int32, (128, 128), 1) < count[0, 0]
    order = slot_order(rows_all, cols_all, 64, valid) + slot_order(cols_all, rows_all, 16, valid)
    for i in range(8):
        table[i:i + 1, :] = order[i]
    idx_copy = pltpu.make_async_copy(table, idx, idx_sem)
    idx_copy.start()

    for b in range(4):
        cott[zh, b] = cot[b * BS:(b + 1) * BS, :].astype(F32).T.astype(BF)
    z_stage("start", 0, K)
    for i in range(2):
        for j in range(4):
            cols = pl.ds(pl.multiple_of((i * 2 + core) * FS, FS), FS)
            wt[i, :, j * FS:(j + 1) * FS] = weight[j * FS:(j + 1) * FS, cols].astype(F32).T.astype(BF)
    x_pass("start", 0)
    cot_send("start")
    idx_copy.wait()
    adj_copy.wait()

    def forward_step(k, _):
        @pl.when(k + 2 < K)
        def _():
            z_own("start", k + 2)
            x_send("start", k + 2, z)
            z_stage("start", k + 2)

        @pl.when(k + 3 == K)
        def _():
            cot_send("start")

        @pl.when(k + 1 < K)
        def _():
            x_pass("start", k + 1)

        @pl.when(k > 0)
        def _():
            def one(p, _):
                y_sum(k - 1, p)
                d_send("start", k - 1, p)
                return 0
            lax.fori_loop(0, NP, one, 0)
        x_last(k)

        forward_tile(k)
        return 0
    lax.fori_loop(0, K, forward_step, 0)

    def last_sum(p, _):
        y_sum(K - 1, p)
        d_send("start", K - 1, p)
        return 0
    lax.fori_loop(0, NP, last_sum, 0)
    blocks(d_pass, "start", K - 2)
    go("recv", cott.at[1 - zh], cott.at[1 - zh], cs.at[0], cr.at[0], to_far)

    def mix_rows(p, dd):
        return gmix.at[pl.ds(p * PB, PB), pl.ds(pl.multiple_of(dd * FS, FS), FS), :]

    def mix_send(op, p):
        go(op, mix_rows(p, d), mix_rows(p, d), gs.at[p, 0], gr.at[p, 0], to_core)
        go(op, mix_rows(p, d_far), mix_rows(p, d_far), gs.at[p, 1], gr.at[p, 1], to_core)

    def mix_last(p):
        go("recv", mix_rows(p, d_core), mix_rows(p, d_core), gs.at[p, 0], gr.at[p, 0], to_core)
        go("recv", mix_rows(p, d_diag), mix_rows(p, d_diag), gs.at[p, 1], gr.at[p, 1], to_core)

    def dense(b):
        for own in (True, False):
            at = zh if own else 1 - zh
            dd = at * 2 + core
            m = jnp.dot(wt[at], agg[b], preferred_element_type=F32)
            sq = m * m
            t = jnp.tanh(GC * (m + 0.044715 * (sq * m)))
            half = 0.5 + 0.5 * t
            if own:
                act_out[b] = (m * half).astype(BF)
            slope = half + 0.5 * m * (1.0 - t * t) * (GC + (3 * 0.044715 * GC) * sq)
            gmix[b, pl.ds(pl.multiple_of(dd * FS, FS), FS), :] = (
                cott[at, b].astype(F32) * slope
            ).astype(BF)

    def back_mix(p):
        mix_last(p)

        def one(q, _):
            b = p * PB + q
            ga = jnp.dot(
                weight[pl.ds(pl.multiple_of(d * FS, FS), FS), :], gmix[b], preferred_element_type=F32
            ).astype(BF)
            for k in range(K):
                tgt[k, c * 4 + b] = ga[k * CH:(k + 1) * CH]
            return 0
        lax.fori_loop(0, PB, one, 0)
        t_send("start", 0, p)

    def t_send(op, k, p):
        own = tgt.at[k, pl.ds(c * 4 + p * PB, PB)]
        for o in range(1, 4):
            go(op, own, own, ts.at[k, p, o], tr.at[k, p, c], {"col": (c + o) % 4})

    def t_last(k):
        def one(p, _):
            for o in range(1, 4):
                src = (c + o) % 4
                ref = tgt.at[k, pl.ds(src * 4 + p * PB, PB)]
                go("recv", ref, ref, ts.at[k, p, o], tr.at[k, p, src], {"col": src})
            return 0
        lax.fori_loop(0, NP, one, 0)

    d_pass("start", K - 1, 0)

    def middle(p, _):
        @pl.when(p < NP - 1)
        def _():
            d_pass("start", K - 1, p + 1)
        for k in range(K):
            d_last(k, p)

        def one(q, _):
            dense(p * PB + q)
            return 0
        lax.fori_loop(0, PB, one, 0)
        mix_send("start", p)

        @pl.when(p > 0)
        def _():
            back_mix(p - 1)
        return 0
    lax.fori_loop(0, NP, middle, 0)
    back_mix(NP - 1)
    for k in range(1, K):
        blocks(t_send, "start", k)

    def gw_block(b, _):
        own = agg[b, pl.ds(pl.multiple_of(d * FS, FS), FS), :]
        for j in range(2):
            add = lax.dot_general(
                own, gmix[b, j * 256:(j + 1) * 256, :], (((1,), (1,)), ((), ())),
                preferred_element_type=F32,
            )
            for q in range(4):
                gw[q, :, j * 256:(j + 1) * 256] += add[q * 32:(q + 1) * 32]
        return 0
    gw[...] = jnp.zeros_like(gw)
    lax.fori_loop(0, 4, gw_block, 0)

    def wy(op, o):
        to = (c + o) % 4
        go(op, gw.at[to], gwy.at[c], wys.at[o], wyr.at[c], {"col": to})

    def wx(op, o):
        to = (x + o) % 4
        go(op, gwx.at[to], gwxr.at[x], wxs.at[o], wxr.at[x], {"row": to * 4 + z})

    def wz(op, o):
        go(op, gwz.at[z], gwz.at[z], wzs.at[o], wzr.at[z], {"row": x * 4 + (z + o) % 4})

    def vx(op, o):
        go(op, gwxa.at[x], gwxa.at[x], vxs.at[o], vxr.at[x], {"row": (x + o) % 4 * 4 + z})

    def vy(op, o):
        own = gw_out.at[pl.ds(pl.multiple_of(c * 32, 32), 32), :]
        go(op, own, own, vys.at[o], vyr.at[c], {"col": (c + o) % 4})

    def all3(fn, op):
        for o in range(1, 4):
            fn(op, o)

    def weight_step(it):
        if it == 1:
            for o in range(1, 4):
                src = (c + o) % 4
                go("recv", gw.at[c], gwy.at[src], wys.at[o], wyr.at[src], {"col": src})
            total = gw[c]
            for o in range(1, 4):
                total = total + gwy[(c + o) % 4]
            for q in range(4):
                gwx[q] = total[q * 8:(q + 1) * 8]
            all3(wx, "start")

        if it == 2:
            for o in range(1, 4):
                src = (x + o) % 4
                go("recv", gwx.at[x], gwxr.at[src], wxs.at[o], wxr.at[src], right)
            total = gwx[x]
            for o in range(1, 4):
                total = total + gwxr[(x + o) % 4]
            gwz[z] = total
            all3(wz, "start")

        if it == 3:
            for o in range(1, 4):
                src = (z + o) % 4
                go("recv", gwz.at[src], gwz.at[src], wzs.at[o], wzr.at[src], up)
            gwxa[x] = (gwz[0] + gwz[1]) + (gwz[2] + gwz[3])
            all3(vx, "start")

        if it == 4:
            for o in range(1, 4):
                src = (x + o) % 4
                go("recv", gwxa.at[src], gwxa.at[src], vxs.at[o], vxr.at[src], right)
            for q in range(4):
                gw_out[pl.ds(pl.multiple_of(c * 32 + q * 8, 8), 8), :] = gwxa[q]
            all3(vy, "start")

    all3(wy, "start")

    def backward_tile(k):
        t_last(k)

        def move(i, _):
            work[i] = tgt[k, i]
            return 0
        lax.fori_loop(0, 16, move, 0, unroll=4)

        def slot(s, acc):
            prod = jnp.dot(work[idx[RB, s]], adj[idx[QB, s]], preferred_element_type=F32)
            acc = acc * idx[KB, s].astype(F32) + prod
            buf[s] = acc.astype(BF)
            return acc
        lax.fori_loop(0, NB, slot, jnp.zeros((CH, BS), F32), unroll=16)

        def pick(i, _):
            last = idx[LB, i]
            on = (jnp.minimum(last, 0) + 1).astype(F32)
            terms[k, i // 16, i // 4 % 4, i % 4] = (buf[jnp.maximum(last, 0)].astype(F32) * on).astype(BF)
            return 0
        lax.fori_loop(0, 64, pick, 0, unroll=4)

    HALF = CH // 2
    order = (3, 0, 2, 1)

    def add_to(ref, at, got):
        ref[at] = (ref[at].astype(F32) + got.astype(F32)).astype(BF)

    def term(k, xx, zz, lo=0, n=CH):
        return terms.at[k, xx, zz, pl.ds(0, 3), pl.ds(lo, n)]

    def far_half(op, k):
        for zz in order:
            go(op, term(k, xop, zz, 0, HALF), xol.at[k, zz], asr.at[k, zz], arl.at[k, zz], right)
            go(op, term(k, xop, zz, HALF, HALF), xor_.at[k, zz], asl.at[k, zz], arr.at[k, zz], left)

    def near_full(op, k):
        for zz in order:
            if op == "start":
                go("recv", term(k, xop, zz, 0, HALF), xol.at[k, zz], asr.at[k, zz], arl.at[k, zz], right)
                for b in range(3):
                    add_to(terms, (k, xr1, zz, b, slice(0, HALF)), xol[k, zz, b])
            go(op, term(k, xr1, zz), xfl.at[k, zz], bsr.at[k, zz], brl.at[k, zz], right)
            if op == "start":
                go("recv", term(k, xop, zz, HALF, HALF), xor_.at[k, zz], asl.at[k, zz], arr.at[k, zz], left)
                for b in range(3):
                    add_to(terms, (k, xl1, zz, b, slice(HALF, CH)), xor_[k, zz, b])
            go(op, term(k, xl1, zz), xfr.at[k, zz], bsl.at[k, zz], brr.at[k, zz], left)

    def x_sum(k):
        for zz in order:
            go("recv", term(k, xr1, zz), xfl.at[k, zz], bsr.at[k, zz], brl.at[k, zz], right)
            go("recv", term(k, xl1, zz), xfr.at[k, zz], bsl.at[k, zz], brr.at[k, zz], left)
            for b in range(3):
                lines[k, zz, b] = (
                    terms[k, x, zz, b].astype(F32) + xfl[k, zz, b].astype(F32) + xfr[k, zz, b].astype(F32)
                ).astype(BF)
            if zz > 0:
                @pl.when(z == 0)
                def _():
                    up_msg("start", k, zz)
            if zz < 3:
                @pl.when(z == 3)
                def _():
                    down_msg("start", k, zz)

    def up_msg(op, k, zz):
        go(op, lines.at[k, zz], zfd.at[k, zz], us.at[k, zz], dnr.at[k, zz], up)

    def down_msg(op, k, zz):
        go(op, lines.at[k, zz], zfu.at[k, zz], dns.at[k, zz], ur.at[k, zz], down)

    def pass_on(op, k):
        for at, zz in ((1, 3), (1, 2), (2, 3)):
            @pl.when(z == at)
            def _():
                if op == "start":
                    up_msg("recv", k, zz)
                    for b in range(3):
                        add_to(lines, (k, zz, b), zfd[k, zz, b])
                up_msg(op, k, zz)

            @pl.when(z == 3 - at)
            def _():
                if op == "start":
                    down_msg("recv", k, 3 - zz)
                    for b in range(3):
                        add_to(lines, (k, 3 - zz, b), zfu[k, 3 - zz, b])
                down_msg(op, k, 3 - zz)

    def x_sum_sent(k):
        for zz in (1, 2, 3):
            @pl.when(z == 0)
            def _():
                up_msg("sent", k, zz)

            @pl.when(z == 3)
            def _():
                down_msg("sent", k, 3 - zz)

    def finish(k):
        rows = pl.ds(k * CH, CH)
        for b in range(3):
            gf_out[b, rows, :] = lines[k, z, b].astype(F32)

        @pl.when(z > 0)
        def _():
            up_msg("recv", k, z)
            for b in range(3):
                gf_out[b, rows, :] += zfd[k, z, b].astype(F32)

        @pl.when(z < 3)
        def _():
            down_msg("recv", k, z)
            for b in range(3):
                gf_out[b, rows, :] += zfu[k, z, b].astype(F32)

    def up3(op, k, zz):
        go(op, terms.at[k, :, zz, 3], z3d.at[k, zz], u3s.at[k, zz], d3r.at[k, zz], up)

    def down3(op, k, zz):
        go(op, terms.at[k, :, zz, 3], z3u.at[k, zz], d3s.at[k, zz], u3r.at[k, zz], down)

    def line3(op, k, stage):
        for zz in range(3, stage, -1):
            @pl.when(z == stage)
            def _():
                if op == "start" and stage > 0:
                    up3("recv", k, zz)
                    for q in range(4):
                        add_to(terms, (k, q, zz, 3), z3d[k, zz, q])
                up3(op, k, zz)

            @pl.when(z == 3 - stage)
            def _():
                if op == "start" and stage > 0:
                    down3("recv", k, 3 - zz)
                    for q in range(4):
                        add_to(terms, (k, q, 3 - zz, 3), z3u[k, 3 - zz, q])
                down3(op, k, 3 - zz)

    def line3_sum(k):
        @pl.when(z > 0)
        def _():
            up3("recv", k, z)
            for q in range(4):
                add_to(terms, (k, q, z, 3), z3d[k, z, q])

        @pl.when(z < 3)
        def _():
            down3("recv", k, z)
            for q in range(4):
                add_to(terms, (k, q, z, 3), z3u[k, z, q])

    def one3(k, xx, lo=0, n=CH):
        return terms.at[k, xx, z, 3, pl.ds(lo, n)]

    def far3(op, k):
        go(op, one3(k, xop, 0, HALF), xo3.at[k, 0], o3s.at[k, 0], o3r.at[k, 0], right)
        go(op, one3(k, xop, HALF, HALF), xo3.at[k, 1], o3s.at[k, 1], o3r.at[k, 1], left)

    def near3(op, k):
        if op == "start":
            go("recv", one3(k, xop, 0, HALF), xo3.at[k, 0], o3s.at[k, 0], o3r.at[k, 0], right)
            add_to(terms, (k, xr1, z, 3, slice(0, HALF)), xo3[k, 0])
        go(op, one3(k, xr1), xf3.at[k, 0], f3s.at[k, 0], f3r.at[k, 0], right)
        if op == "start":
            go("recv", one3(k, xop, HALF, HALF), xo3.at[k, 1], o3s.at[k, 1], o3r.at[k, 1], left)
            add_to(terms, (k, xl1, z, 3, slice(HALF, CH)), xo3[k, 1])
        go(op, one3(k, xl1), xf3.at[k, 1], f3s.at[k, 1], f3r.at[k, 1], left)

    def finish3(k):
        go("recv", one3(k, xr1), xf3.at[k, 0], f3s.at[k, 0], f3r.at[k, 0], right)
        go("recv", one3(k, xl1), xf3.at[k, 1], f3s.at[k, 1], f3r.at[k, 1], left)
        gf_out[3, k * CH:(k + 1) * CH, :] = (
            terms[k, x, z, 3].astype(F32) + xf3[k, 0].astype(F32) + xf3[k, 1].astype(F32)
        )

    backward_tile(0)
    far_half("start", 0)
    line3("start", 0, 0)
    backward_tile(1)
    line3("start", 1, 0)
    line3("start", 0, 1)
    near_full("start", 0)
    far_half("start", 1)
    line3("start", 0, 2)
    weight_step(1)
    line3("start", 1, 1)
    line3_sum(0)
    far3("start", 0)
    line3("start", 1, 2)
    x_sum(0)
    near_full("start", 1)
    near3("start", 0)
    line3_sum(1)
    far3("start", 1)
    weight_step(2)
    pass_on("start", 0)
    near3("start", 1)
    finish3(0)
    weight_step(3)
    finish(0)
    finish3(1)
    weight_step(4)
    def drain(k, _):
        z_own("sent", k)
        x_send("sent", k, z)
        z_stage("sent", k)
        x_pass("sent", k)
        for fn in (y_send, d_send, d_pass, t_send):
            blocks(fn, "sent", k)
        far_half("sent", k)
        for stage in range(3):
            line3("sent", k, stage)
        far3("sent", k)
        near3("sent", k)
        return 0
    lax.fori_loop(0, K, drain, 0)
    near_full("sent", 0)
    x_sum_sent(0)
    pass_on("sent", 0)
    blocks(mix_send, "sent")
    cot_send("sent")
    for fn in (wy, wx, wz, vx):
        all3(fn, "sent")

    x_sum(1)
    pass_on("start", 1)
    finish(1)

    for o in range(1, 4):
        src = (c + o) % 4
        ref = gw_out.at[pl.ds(pl.multiple_of(src * 32, 32), 32), :]
        go("recv", ref, ref, vys.at[o], vyr.at[src], {"col": src})

    near_full("sent", K - 1)
    x_sum_sent(K - 1)
    pass_on("sent", K - 1)
    all3(vy, "sent")


def write_out(act_t, gf_t, gw, act, gf, gw_out):
    gw_out[...] = gw[...]
    for b in range(4):
        act[b * BS:(b + 1) * BS, :] = act_t[b].astype(F32).T.astype(BF)
        gf[b * BS:(b + 1) * BS, :] = gf_t[b].T.astype(BF)


def layer(features, weight, cotangent, adjacency_blocks, block_rows, block_cols, tile_counts):
    blocks = adjacency_blocks[0, 0]
    vm = pl.BlockSpec(memory_space=pltpu.VMEM)
    dma = lambda *s: pltpu.SemaphoreType.DMA(s)
    per_chunk = (K, 4)
    scratch = [
        pltpu.SMEM((8, 128), jnp.int32),
        pltpu.VMEM((8, 128), jnp.int32),
        pltpu.SemaphoreType.DMA,
        pltpu.VMEM((NB, BS, BS), BF),
        pltpu.VMEM((K, 64, CH, BS), BF),
        pltpu.VMEM((64, CH, BS), BF),
        pltpu.VMEM((NB, CH, BS), BF),
        pltpu.VMEM((K, 16, CH, BS), BF),
        pltpu.VMEM((K, 4, 4, CH, BS), BF),
        pltpu.VMEM((4, 512, BS), BF),
        pltpu.VMEM((2, 4, FS, BS), BF),
        pltpu.VMEM((4, 512, BS), BF),
        pltpu.VMEM((2, FS, 512), BF),
        pltpu.VMEM((K, 16, CH, BS), BF),
        pltpu.VMEM((K, 4, 4, 4, CH, BS), BF),
        pltpu.VMEM((K, 4, 3, CH, BS), BF),
        pltpu.VMEM((K, 4, 3, CH, BS), BF),
        pltpu.VMEM((K, 4, 3, CH // 2, BS), BF),
        pltpu.VMEM((K, 4, 3, CH // 2, BS), BF),
        pltpu.VMEM((K, 4, 3, CH, BS), BF),
        pltpu.VMEM((K, 4, 3, CH, BS), BF),
        pltpu.VMEM((K, 4, 3, CH, BS), BF),
        pltpu.VMEM((K, 4, 4, CH, BS), BF),
        pltpu.VMEM((K, 4, 4, CH, BS), BF),
        pltpu.VMEM((K, 2, CH // 2, BS), BF),
        pltpu.VMEM((K, 2, CH, BS), BF),
        pltpu.VMEM((4, 32, 512), F32),
        pltpu.VMEM((4, 32, 512), F32),
        pltpu.VMEM((4, 8, 512), F32),
        pltpu.VMEM((4, 8, 512), F32),
        pltpu.VMEM((4, 8, 512), F32),
        pltpu.VMEM((4, 8, 512), F32),
        pltpu.SemaphoreType.DMA,
    ]
    scratch += [dma(*per_chunk) for _ in range(11)]
    scratch += [dma(K, 4, 4), dma(K, 4, 4), dma(K, 4, 3), dma(K, 4, 3), dma(1), dma(1), dma(4, 2), dma(4, 2)]
    scratch += [dma(K, 4, 4), dma(K, 4, 4)]
    scratch += [dma(*per_chunk) for _ in range(16)] + [dma(K, 2) for _ in range(4)]
    scratch += [dma(4) for _ in range(10)]
    act_t, gf_t, grad_weight = pl.pallas_call(
        kernel,
        out_shape=(
            jax.ShapeDtypeStruct((4, FS, BS), BF),
            jax.ShapeDtypeStruct((4, FS, BS), F32),
            jax.ShapeDtypeStruct((FS, 512), F32),
        ),
        in_specs=[pl.BlockSpec(memory_space=pltpu.SMEM)] + [vm] * 5 + [pl.BlockSpec(memory_space=pl.ANY)],
        out_specs=(vm, vm, vm),
        scratch_shapes=scratch,
        compiler_params=pltpu.CompilerParams(
            collective_id=0, has_side_effects=True, vmem_limit_bytes=56 << 20
        ),
        cost_estimate=pl.CostEstimate(flops=4_000_000_000, bytes_accessed=13_000_000, transcendentals=300_000),
    )(tile_counts, block_rows[0], block_cols[0], features, weight, cotangent, blocks)
    return pl.pallas_call(
        write_out,
        out_shape=(
            jax.ShapeDtypeStruct(features.shape, BF),
            jax.ShapeDtypeStruct(features.shape, BF),
            jax.ShapeDtypeStruct((FS, 512), F32),
        ),
        in_specs=[vm] * 3,
        out_specs=(vm, vm, vm),
        cost_estimate=pl.CostEstimate(flops=0, bytes_accessed=2_000_000, transcendentals=0),
    )(act_t, gf_t, grad_weight)


def solution(mesh):
    in_specs = (
        P(("row", "col"), "depth"),
        P(),
        P(("row", "col"), "depth"),
        P("row", "col", None, None, None),
        P("row", "col", None),
        P("row", "col", None),
        P("row", "col"),
    )
    out_specs = (P(("row", "col"), "depth"), P(("row", "col"), "depth"), P("depth", None))
    return jax.shard_map(layer, mesh=mesh, in_specs=in_specs, out_specs=out_specs, check_vma=False)
```
